32 devices in a mesh: facet: 8 (over y, x, core), band: 4 (over z).
Axes of the slice: x: 2, y: 2, z: 4, core: 2. Of those that a mesh axis runs over, the one named last changes fastest.
Arguments:
- visibility: bfloat16 [8, 256, 64, 64], P('band', 'facet'), may hold values from -6 to 6
- uv_positions: int32 [8, 256, 2, 64], P('band', 'facet'), may hold values from 0 to 248
- destinations: int32 [8, 256, 1], P('band', 'facet'), may hold values from 0 to 7; in each aligned block of 32 rows (0 to 31, 32 to 63, ..., all dimensions but the last counted through in order) at most 8 rows name the same one
- column_slots: int32 [8, 256], P('band', 'facet'), may hold values from 0 to 1
- image_cube: float32 [8, 256, 3072], P('band', None, 'facet'), may hold values from 0 to 1
- dual_cube: float32 [8, 256, 3072], P('band', None, 'facet'), may hold values from -2 to 2
- step_sizes: float32 [8], P('band'), may hold values from 0.05 to 0.2
- conv_first: bfloat16 [64, 8, 3, 3], replicated, may hold values from -0.75 to 0.75
- conv_middle: bfloat16 [64, 64, 3, 3], replicated, may hold values from -0.25 to 0.25
- conv_last: bfloat16 [8, 64, 3, 3], replicated, may hold values from -0.25 to 0.25
Outputs:
- image_next: float32 [8, 256, 3072], P('band', None, 'facet')
- dual_next: float32 [8, 256, 3072], P('band', None, 'facet')
The draws below stay inside these ranges and needn't reach their ends.
Inputs may be any that keep to these rules, and one draw needn't show every extreme that they name: `destinations`: in each aligned block of 32 rows (the blocks of one subband held by one device), no facet is named by more than 8 rows, a bound that some block reaches.
All inputs are finite; a program needn't handle non-finite values.
Results may differ from the reference program's by a relative error of at most 0.0067.
Values may be sent and summed in bfloat16 or wider, within the bound.
No kernel may reach another device: no remote copies, remote signals or barrier semaphores. Data moves between devices by JAX's collectives and lax.ppermute only.
A program may use at most 128 MiB of HBM per device.

```python
import math
import jax
import jax.numpy as jnp
import numpy as np
from jax import lax

SUB = 8
P_SIZE = 256
KW = 8
S = 64
CH = 64
FW = 384
BLK_DEV = 32
BLOCKS = 256
CAP = 8
NPOS = 2
NX = 3072
N_FACET = 8


def plant(values, rng, least, high):
    place = [jax.random.randint(jax.random.fold_in(rng, axis), (), 0, length) for axis, length in enumerate(values.shape)]
    longest = values.shape.index(max(values.shape))
    next_to = place[:longest] + [(place[longest] + 1) % values.shape[longest]] + place[longest + 1:]
    return values.at[tuple(place)].set(least).at[tuple(next_to)].set(high)


def block_levels(stream_key, extent, cuts, low, largest):
    factor_of = 1.0
    for dim, blocks in cuts:
        draws = jax.random.uniform(jax.random.fold_in(jax.random.fold_in(stream_key, 6), dim), (blocks,), jnp.float32, low / len(cuts), largest / len(cuts))
        factor_of = factor_of * jnp.repeat(jnp.exp(draws), extent[dim] // blocks).reshape((-1,) + (1,) * (len(extent) - 1 - dim))
    return factor_of


def routed_block(key, own, number, rows, number_of, top, reach, skew):
    ranking = jax.random.permutation(key, number_of)
    crowded, usual = portions_of(number_of, rows * top, reach, skew, True), portions_of(number_of, rows * top, reach, skew, False)
    places = jnp.arange(number_of)

    def named(sizes, offset_by):
        used = int((sizes > 0).sum())
        fixed = max(1, used // 4)
        passed = fixed + (places - fixed + offset_by * (used - fixed)) % max(1, number_of - fixed)
        return jnp.zeros((number_of,), jnp.int32).at[ranking[jnp.where(places < fixed, places, passed)]].set(jnp.asarray(sizes, jnp.int32))

    sizes = jnp.where(number % 4 == 0, named(crowded, number // 4), named(usual, number - number // 4 - 1))
    mixed = jax.random.permutation(jax.random.fold_in(own, 3), number_of)
    source_of, receiver = mixed[0:number_of // 2 * 2:2], mixed[1:number_of // 2 * 2:2]
    room = jnp.minimum(sizes[source_of] - 1, reach - sizes[receiver]) // 2
    room = jnp.where((source_of == ranking[0]) | (receiver == ranking[0]) | (sizes[receiver] == 0), 0, jnp.maximum(room, 0))
    passed = jax.random.randint(jax.random.fold_in(own, 4), (number_of // 2,), 0, 1 << 20) % (room + 1)
    sizes = sizes.at[source_of].add(-passed).at[receiver].add(passed)
    members = jnp.searchsorted(jnp.cumsum(sizes), jnp.arange(rows * top), side="right").astype(jnp.int32)
    table = members.reshape(top, rows).T
    table = table[jax.random.permutation(jax.random.fold_in(own, 1), rows)]
    offset_by = jax.random.randint(jax.random.fold_in(own, 2), (rows, 1), 0, top)
    return jnp.take_along_axis(table, (jnp.arange(top)[None, :] + offset_by) % top, axis=1)


def portions_of(amount, total, limit, skew, full):
    loads = [(1 << 20) // math.isqrt(standing ** skew) + 1 for standing in range(1, amount + 1)]
    largest = limit if full else min(limit, max(-(-total // amount), total * loads[0] // sum(loads)))
    least = 1 if total - largest >= amount - 1 else 0
    given, spare = [largest] + [least] * (amount - 1), total - largest - least * (amount - 1)
    while spare > 0:
        free = [i for i in range(1, amount) if given[i] < largest] or [i for i in range(1, amount) if given[i] < limit]
        whole, left = sum([loads[i] for i in free]), spare
        for i in free:
            extra = min(limit - given[i], max(1, left * loads[i] // whole), spare)
            given[i] = given[i] + extra
            spare = spare - extra
    return np.array(given)


def scatter_about(stream_key, shape, width, limit, pieces=(), held_as=jnp.bfloat16):
    factor_of = block_levels(stream_key, shape, pieces, -0.22, 0.18) if pieces else 1.0
    result = jax.random.normal(stream_key, shape, jnp.float32) * width * factor_of
    return jnp.minimum(jnp.maximum(result, -limit), limit).astype(held_as)


def setup_inputs(seed: int = 0) -> dict:
    key_list = jax.random.split(jax.random.key(seed), 11)
    visibility = scatter_about(key_list[0], (SUB, BLOCKS, S, S), 1.0, 6.0, ((0, 4), (1, 8)))
    uv_positions = plant(jax.random.randint(key_list[1], (SUB, BLOCKS, 2, S), 0, P_SIZE - KW + 1), jax.random.fold_in(key_list[1], 1), 0, P_SIZE - KW).astype(jnp.int32)
    destinations_keys = jax.random.split(jax.random.fold_in(key_list[2], 1), SUB * BLOCKS // BLK_DEV)
    destinations_turns = jax.random.permutation(jax.random.fold_in(key_list[2], 3), SUB * BLOCKS // BLK_DEV)
    destinations = jax.vmap(lambda own, number: routed_block(jax.random.fold_in(key_list[2], 2), own, number, BLK_DEV, N_FACET, 1, CAP, 2))(destinations_keys, destinations_turns).reshape((SUB, BLOCKS, 1))
    column_slots = plant(jax.random.randint(key_list[3], (SUB, BLOCKS), 0, NPOS), jax.random.fold_in(key_list[3], 1), 0, NPOS - 1).astype(jnp.int32)
    image_cube = jnp.clip(1.0 * jax.random.uniform(key_list[4], (SUB, P_SIZE, NX), jnp.float32) ** block_levels(key_list[4], (SUB, P_SIZE, NX), ((0, 4), (2, 8)), -0.2, 0.2), 0.0, 1.0)
    dual_cube = scatter_about(key_list[5], (SUB, P_SIZE, NX), 0.3, 2.0, ((0, 4), (2, 8)), jnp.float32)
    step_sizes = jnp.clip(jnp.exp(math.log(0.2) - 1.3862944 * jax.random.uniform(key_list[6], (SUB,), jnp.float32) ** block_levels(key_list[6], (SUB,), ((0, 4),), -0.2, 0.2)), 0.05, 0.2)
    conv_first = scatter_about(key_list[7], (CH, SUB, 3, 3), (9 * SUB) ** -0.5, 0.75)
    conv_middle = scatter_about(key_list[8], (CH, CH, 3, 3), (9 * CH) ** -0.5, 0.25)
    conv_last = scatter_about(key_list[9], (SUB, CH, 3, 3), (9 * CH) ** -0.5, 0.25)
    return dict(visibility=visibility, uv_positions=uv_positions, destinations=destinations, column_slots=column_slots, image_cube=image_cube, dual_cube=dual_cube, step_sizes=step_sizes, conv_first=conv_first, conv_middle=conv_middle, conv_last=conv_last)


def kernel_matrix(positions):
    cell_index = jnp.arange(P_SIZE, dtype=jnp.float32)
    offset = cell_index[None, :] - positions[:, None]
    centre = (KW - 1) / 2.0
    spread = KW / 4.0
    tap_values = jnp.exp(-0.5 * ((offset - centre) / spread) ** 2)
    inside = (offset >= 0.0) & (offset < KW)
    return jnp.where(inside, tap_values, 0.0).astype(jnp.bfloat16)


def block_panels(group):
    vis_group, pos_group = group
    rows_kernel = jax.vmap(kernel_matrix)(pos_group[:, 0])
    cols_kernel = jax.vmap(kernel_matrix)(pos_group[:, 1])
    half_product = jnp.einsum("gab,gbj->gaj", vis_group.astype(jnp.float32), cols_kernel.astype(jnp.float32)).astype(jnp.bfloat16)
    return jnp.einsum("gai,gaj->gij", rows_kernel.astype(jnp.float32), half_product.astype(jnp.float32)).astype(jnp.bfloat16)


def add_panel(grid, item):
    panel, column = item
    zero_row = jnp.zeros((), jnp.int32)
    current = lax.dynamic_slice(grid, (zero_row, column), (P_SIZE, P_SIZE))
    return lax.dynamic_update_slice(grid, current + panel.astype(jnp.float32), (zero_row, column)), None


def convolve(field, kernel, dilation):
    return lax.conv_general_dilated(field, kernel, (1, 1), [(dilation, dilation), (dilation, dilation)], rhs_dilation=(dilation, dilation), dimension_numbers=("NCHW", "OIHW", "NCHW"), preferred_element_type=jnp.float32)


def reference(visibility, uv_positions, destinations, column_slots, image_cube, dual_cube, step_sizes, conv_first, conv_middle, conv_last):
    gradient_list = []
    for subband in range(SUB):
        vis_groups = visibility[subband].reshape(BLOCKS // BLK_DEV, BLK_DEV, S, S)
        pos_groups = uv_positions[subband].astype(jnp.float32).reshape(BLOCKS // BLK_DEV, BLK_DEV, 2, S)
        panel_set = lax.map(block_panels, (vis_groups, pos_groups)).reshape(BLOCKS, P_SIZE, P_SIZE)
        starts = (destinations[subband, :, 0] * FW + column_slots[subband] * (P_SIZE // 2)).astype(jnp.int32)
        grid, _ = lax.scan(add_panel, jnp.zeros((P_SIZE, NX), jnp.float32), (panel_set, starts))
        gradient_list.append(grid)
    gradient = jnp.stack(gradient_list)
    stepped = image_cube - step_sizes[:, None, None] * gradient
    shifted = stepped + dual_cube
    denoise_in = shifted.astype(jnp.bfloat16)[None]
    hidden_one = jnp.maximum(convolve(denoise_in, conv_first, 1), 0.0).astype(jnp.bfloat16)
    hidden_two = jnp.maximum(convolve(hidden_one, conv_middle, 2), 0.0).astype(jnp.bfloat16)
    noise = convolve(hidden_two, conv_last, 1).astype(jnp.bfloat16)[0]
    image_next = jnp.maximum(shifted - noise.astype(jnp.float32), 0.0)
    dual_next = dual_cube + stepped - image_next
    return image_next, dual_next
```

```python
import jax
import jax.numpy as jnp
from jax import lax
from jax.experimental import pallas as pl
from jax.experimental.pallas import tpu as pltpu
from jax.sharding import PartitionSpec as P

P_SIZE = 256
KW = 8
S = 64
HALF = P_SIZE // 2
CENTRE = (P_SIZE - KW + HALF) // 2
HALO = 4
PAD = 8
GROUP = 8
CH = 64
BF = jnp.bfloat16
F32 = jnp.float32


def params(mib=48):
    return pltpu.CompilerParams(vmem_limit_bytes=mib << 20)


def vmem():
    return pl.BlockSpec(memory_space=pltpu.VMEM)


def smem():
    return pl.BlockSpec(memory_space=pltpu.SMEM)


def pack_blocks(visibility, uv_positions, destinations, column_slots, facets, pairs):
    subs, blocks = visibility.shape[:2]
    vis_rows = subs * pairs * S
    pos_rows = -(-2 * subs * pairs // 16) * 16

    def kernel(dest_ref, slot_ref, vis_ref, pos_ref, out_ref, count_ref, place_ref):
        out_ref[...] = jnp.zeros(out_ref.shape, BF)
        place_ref[...] = jnp.zeros(place_ref.shape, F32)
        for n in range(subs * facets):
            count_ref[n] = 0
        lane = lax.broadcasted_iota(jnp.int32, (1, 2 * S), 1) // S

        def one(n, carry):
            for sub in range(subs):
                facet = dest_ref[sub, n, 0]
                slot = slot_ref[sub, n]
                count = count_ref[sub * facets + facet]
                count_ref[sub * facets + facet] = count + 1
                pair = count // 2
                side = count - 2 * pair
                half_mask = jnp.where(lane == side, 1.0, 0.0).astype(BF)
                block = vis_ref[sub, n]
                wide = jnp.concatenate([block, block], axis=1) * half_mask
                row = pl.multiple_of((sub * pairs + pair) * S, S)
                out_ref[facet, pl.ds(row, S), :] += wide
                where = facet * pos_rows + sub * pairs + pair
                place = pos_ref[sub, n].astype(F32)
                shift = (slot * HALF - CENTRE).astype(F32)
                place_ref[side, pl.ds(where, 1), :] = place[0:1]
                place_ref[side, pl.ds(where + subs * pairs, 1), :] = place[1:2] + shift
            return carry

        lax.fori_loop(0, blocks, one, 0)
        both = jnp.concatenate([place_ref[0], place_ref[1]], axis=1).astype(BF)
        out_ref[:, vis_rows:, :] = both.reshape(facets, pos_rows, 2 * S)

    return pl.pallas_call(
        kernel,
        out_shape=jax.ShapeDtypeStruct((facets, vis_rows + pos_rows, 2 * S), BF),
        in_specs=[smem(), smem(), vmem(), vmem()],
        out_specs=vmem(),
        scratch_shapes=[
            pltpu.SMEM((subs * facets,), jnp.int32),
            pltpu.VMEM((2, facets * pos_rows, S), F32),
        ],
        compiler_params=params(),
        name="pack_blocks",
    )(destinations, column_slots, visibility, uv_positions)


def taps(row, col):
    offset = col - row
    value = jnp.exp(-0.5 * ((offset.astype(F32) - (KW - 1) / 2.0) / (KW / 4.0)) ** 2)
    return jnp.where((offset >= 0) & (offset < KW), value, 0.0).astype(BF)


def contract_last(a, b):
    return lax.dot_general(a, b, (((1,), (1,)), ((), ())), preferred_element_type=F32)


def contract_first(a, b):
    return lax.dot_general(a, b, (((0,), (0,)), ((), ())), preferred_element_type=F32)


def dot(a, b):
    return jnp.dot(a, b, preferred_element_type=F32)


def grid_and_step(received, image, dual, steps, pairs, bands):
    facets = received.shape[0]
    subs, rows, width = image.shape
    vis_rows = subs * pairs * S
    per = 4
    sources = per // pairs
    band_rows = rows // bands
    piece = band_rows + 2 * HALO

    def kernel(step_ref, rec_ref, img_ref, dual_ref, shift_ref, edge_l, edge_r, *rest):
        piece_refs = rest[:bands]
        acc_ref, den_ref = rest[bands:]
        acc_ref[...] = jnp.zeros(acc_ref.shape, F32)
        lane = lax.broadcasted_iota(jnp.int32, (1, 2 * S), 1)
        left = jnp.where(lane < S, 1.0, 0.0).astype(BF)
        right = jnp.where(lane < S, 0.0, 1.0).astype(BF)
        zero = jnp.zeros((2 * S, 2 * S), BF)
        row_id = lax.broadcasted_iota(jnp.int32, (rows, 2 * S), 0).astype(F32)
        col_id = lax.broadcasted_iota(jnp.int32, (width, 2 * S), 0).astype(F32) - CENTRE

        def one(it, carry):
            for sub in range(subs):
                first, second = [], []
                for q in range(per):
                    source = it * sources + q // pairs
                    pair = q % pairs
                    block = rec_ref[source, pl.ds((sub * pairs + pair) * S, S), :]
                    diag = jnp.concatenate([block * left, block * right], axis=0)
                    place = rec_ref[source, vis_rows : vis_rows + 16, :].astype(F32)
                    at = sub * pairs + pair
                    u_row = place[at : at + 1]
                    v_row = place[at + subs * pairs : at + subs * pairs + 1]
                    u_hot = jnp.where(row_id == u_row, 1.0, 0.0).astype(BF)
                    v_hot = jnp.where(col_id == v_row, 1.0, 0.0).astype(BF)
                    first.append((u_hot, diag))
                    second.append(v_hot)
                spread = []
                for q in range(0, per, 2):
                    hot = jnp.concatenate([first[q][0], first[q + 1][0]], axis=1)
                    block = jnp.concatenate(
                        [
                            jnp.concatenate([first[q][1], zero], axis=1),
                            jnp.concatenate([zero, first[q + 1][1]], axis=1),
                        ],
                        axis=0,
                    )
                    spread.append(dot(hot, block).astype(BF))
                acc_ref[sub] += contract_last(
                    jnp.concatenate(spread, axis=1), jnp.concatenate(second, axis=1)
                )
            return carry

        lax.fori_loop(0, facets // sources, one, 0)
        u_taps = taps(
            lax.broadcasted_iota(jnp.int32, (rows, rows), 1),
            lax.broadcasted_iota(jnp.int32, (rows, rows), 0),
        )
        v_taps = taps(
            lax.broadcasted_iota(jnp.int32, (width, width), 0),
            lax.broadcasted_iota(jnp.int32, (width, width), 1),
        )
        den_ref[...] = jnp.zeros(den_ref.shape, F32)
        me = lax.axis_index("band")
        for sub in range(subs):
            total = acc_ref[sub]
            high = total.astype(BF)
            low = (total - high.astype(F32)).astype(BF)
            half = dot(u_taps, high) + dot(u_taps, low)
            gradient = dot(half.astype(BF), v_taps)
            stepped = img_ref[sub] - step_ref[sub] * gradient
            shifted = stepped + dual_ref[sub]
            shift_ref[sub] = shifted
            den_ref[sub, HALO : HALO + rows, :] = shifted
        for k in range(bands):
            start = pl.multiple_of(lax.rem(me + k, bands) * band_rows, band_rows)
            piece_refs[k][...] = jnp.concatenate(
                [den_ref[sub, pl.ds(start, piece), :] for sub in range(subs)], axis=0
            ).astype(BF)
        pick_row = lax.broadcasted_iota(jnp.int32, (subs * HALO, HALF), 0)
        pick_lane = lax.broadcasted_iota(jnp.int32, (subs * HALO, HALF), 1)
        for k in range(bands):
            for ref, at, base in ((edge_l, 0, 0), (edge_r, width - HALF, HALF - HALO)):
                total = None
                for sub in range(subs):
                    pick = jnp.where(
                        (pick_row // HALO == sub) & (pick_lane == base + pick_row % HALO), 1.0, 0.0
                    ).astype(BF)
                    part = den_ref[sub, k * band_rows : k * band_rows + HALF, at : at + HALF].astype(BF)
                    term = contract_last(pick, part)
                    total = term if total is None else total + term
                ref[k] = total.astype(BF)

    edge = jax.ShapeDtypeStruct((bands, subs * HALO, HALF), BF)
    return pl.pallas_call(
        kernel,
        out_shape=[jax.ShapeDtypeStruct(image.shape, F32), edge, edge]
        + [jax.ShapeDtypeStruct((subs * piece, width), BF)] * bands,
        in_specs=[smem(), vmem(), vmem(), vmem()],
        out_specs=[vmem()] * (3 + bands),
        scratch_shapes=[
            pltpu.VMEM((subs, rows, width), F32),
            pltpu.VMEM((subs, (bands - 1) * band_rows + HALF, width), F32),
        ],
        compiler_params=params(),
        name="grid_and_step",
    )(steps, received, image, dual)


def toeplitz(weights, outs, ins):
    w = weights.transpose(3, 2, 1, 0)
    cols = [jnp.pad(w, ((0, 0), (o, ins - 3 - o), (0, 0), (0, 0))) for o in range(outs)]
    return jnp.stack(cols, axis=3)


def weight_matrices(conv_first, conv_middle, conv_last):
    first = toeplitz(conv_first, GROUP, GROUP + 2)
    ci = conv_first.shape[1]
    first = first.reshape(3 * (GROUP + 2) * ci, GROUP // 2, 2, CH)
    first = first.transpose(0, 2, 1, 3).reshape(3 * (GROUP + 2) * ci, GROUP * CH)
    middle = toeplitz(conv_middle, GROUP // 2, GROUP // 2 + 2).reshape(
        3 * (GROUP // 2 + 2) * CH, GROUP // 2 * CH
    )
    last = toeplitz(conv_last, GROUP, GROUP + 2)
    co = conv_last.shape[0]
    last = last.transpose(1, 2, 0, 4, 3).reshape(GROUP + 2, CH, 3 * co * GROUP)
    main = last[:GROUP].reshape(GROUP // 2, 2, CH, -1).transpose(1, 0, 2, 3)
    main = main.reshape(GROUP * CH, 3 * co * GROUP)
    tail = jnp.pad(last[GROUP:], ((0, 0), (0, CH), (0, 0))).reshape(4 * CH, 3 * co * GROUP)
    return first, middle, jnp.concatenate([main, tail], axis=0)


def denoise(pieces, edges, first, middle, last, subs, bands, band_rows, width):
    channels = subs * bands
    piece = band_rows + 2 * HALO
    groups = band_rows // GROUP + 1
    cols = width + 2 * PAD
    lanes = -(-cols // 128) * 128
    tall = -(-(cols + 2 * HALO) // 16) * 16
    in_rows = GROUP + 2
    facets = lax.axis_size("facet")

    def kernel(first_ref, mid_ref, last_ref, *rest):
        piece_refs = rest[:bands]
        edge_refs = rest[bands : 2 * bands]
        out_refs = rest[2 * bands : 3 * bands]
        x_ref, one_ref, two_ref, noise_ref = rest[3 * bands :]
        me = lax.axis_index("band")
        facet = lax.axis_index("facet")
        x_ref[:, piece * channels :, :] = jnp.zeros((lanes // 128, 2 * channels, 128), F32)
        one_ref[groups] = jnp.zeros(one_ref.shape[1:], BF)
        place_row = lax.broadcasted_iota(jnp.int32, (2 * subs * HALO, lanes), 0)
        place_lane = lax.broadcasted_iota(jnp.int32, (2 * subs * HALO, lanes), 1)
        side = place_row // (subs * HALO)
        spot = jnp.where(side == 0, PAD - HALO, PAD + width) + place_row % HALO
        for k in range(bands):
            band = lax.rem(me + bands - k, bands)
            for sub in range(subs):
                put = jnp.where(
                    (place_lane == spot) & (place_row // HALO % subs == sub), 1.0, 0.0
                ).astype(BF)
                halo = contract_first(edge_refs[k][...], put)[:piece]
                own = piece_refs[k][sub * piece : (sub + 1) * piece, :].astype(F32)
                own = jnp.concatenate([own, jnp.zeros((piece, lanes - width), F32)], axis=1)
                own = pltpu.roll(own, PAD, 1) + halo
                for part in range(lanes // 128):
                    x_ref[part, pl.ds(band * subs + sub, piece, stride=channels), :] = own[
                        :, part * 128 : (part + 1) * 128
                    ]

        col = lax.broadcasted_iota(jnp.int32, (1, lanes), 1) - PAD
        inside = ((col >= 0) | (facet > 0)) & ((col < width) | (facet < facets - 1))
        inside = jnp.where(inside, 1.0, 0.0)
        lane_id = lax.broadcasted_iota(jnp.int32, (1, GROUP * CH), 1)
        lane_row = lane_id // (GROUP // 2 * CH) + 2 * (lane_id // CH % (GROUP // 2))

        def layer_one(g, carry):
            top = pl.multiple_of(g * GROUP * channels, GROUP)
            x = jnp.concatenate(
                [x_ref[part, pl.ds(top, in_rows * channels), :] for part in range(lanes // 128)], axis=1
            )
            stack = jnp.concatenate(
                [pltpu.roll(x, 1, 1) * inside, x * inside, pltpu.roll(x, lanes - 1, 1) * inside], axis=0
            )
            stack = stack.astype(BF).T[:cols]
            hidden = dot(stack, first_ref[...])
            row = lane_row + (g * GROUP + 1 - HALO) + me * band_rows
            keep = jnp.where((row >= 0) & (row < band_rows * bands), 1.0, 0.0)
            one_ref[g, 0:cols, :] = (jnp.maximum(hidden, 0.0) * keep).astype(BF)
            return carry

        lax.fori_loop(0, groups, layer_one, 0)
        block = GROUP // 2 * CH

        def layer_two(g, carry):
            row = lane_row + (g * GROUP - 1) + me * band_rows
            keep = jnp.where((row >= 0) & (row < band_rows * bands), 1.0, 0.0)
            for phase in range(2):
                here = one_ref[g, :, phase * block : (phase + 1) * block]
                after = one_ref[g + 1, :, phase * block : phase * block + 2 * CH]
                parts = []
                for t in range(3):
                    parts += [here[2 * t : 2 * t + cols], after[2 * t : 2 * t + cols]]
                hidden = dot(jnp.concatenate(parts, axis=1), mid_ref[...])
                part = keep[:, phase * block : (phase + 1) * block]
                two_ref[g, :, phase * block : (phase + 1) * block] = (
                    jnp.maximum(hidden, 0.0) * part
                ).astype(BF)
            return carry

        lax.fori_loop(0, groups, layer_two, 0)
        out_ch = channels * GROUP
        out_col = lax.broadcasted_iota(jnp.int32, (1, width), 1)
        has_left = jnp.where((out_col > 0) | (facet > 0), 1.0, 0.0)
        has_right = jnp.where((out_col < width - 1) | (facet < facets - 1), 1.0, 0.0)

        def layer_three(g, carry):
            hidden = jnp.concatenate(
                [
                    two_ref[g],
                    two_ref[g + 1, :, 0 : 2 * CH],
                    two_ref[g + 1, :, block : block + 2 * CH],
                ],
                axis=1,
            )
            y = dot(hidden, last_ref[...]).T
            base = PAD - 2
            noise = (
                y[:out_ch, base - 1 : base - 1 + width] * has_left
                + y[out_ch : 2 * out_ch, base : base + width]
                + y[2 * out_ch :, base + 1 : base + 1 + width] * has_right
            )
            noise_ref[:, pl.ds(pl.multiple_of(g * GROUP, GROUP), GROUP), :] = noise.reshape(
                channels, GROUP, width
            )
            return carry

        lax.fori_loop(0, groups - 1, layer_three, 0)
        for k in range(bands):
            band = lax.rem(me + k, bands)
            for sub in range(subs):
                out_refs[k][sub * band_rows : (sub + 1) * band_rows, :] = noise_ref[
                    band * subs + sub
                ].astype(BF)

    return pl.pallas_call(
        kernel,
        out_shape=[jax.ShapeDtypeStruct((subs * band_rows, width), BF)] * bands,
        in_specs=[vmem()] * (3 + 2 * bands),
        out_specs=[vmem()] * bands,
        scratch_shapes=[
            pltpu.VMEM((lanes // 128, (groups * GROUP + 2) * channels, 128), F32),
            pltpu.VMEM((groups + 1, tall, GROUP * CH), BF),
            pltpu.VMEM((groups, cols, GROUP * CH), BF),
            pltpu.VMEM((channels, band_rows, width), F32),
        ],
        compiler_params=params(),
        name="denoise",
    )(first, middle, last, *pieces, *edges)


def finish(shifted, noises, bands):
    subs, rows, width = shifted.shape
    band_rows = rows // bands

    def kernel(shift_ref, *rest):
        noise_refs = rest[:bands]
        img_ref, dual_ref = rest[bands:]
        me = lax.axis_index("band")
        for k in range(bands):
            start = pl.multiple_of(lax.rem(me + bands - k, bands) * band_rows, band_rows)
            for sub in range(subs):
                noise = noise_refs[k][sub * band_rows : (sub + 1) * band_rows, :].astype(F32)
                shifted_part = shift_ref[sub, pl.ds(start, band_rows), :]
                image_next = jnp.maximum(shifted_part - noise, 0.0)
                img_ref[sub, pl.ds(start, band_rows), :] = image_next
                dual_ref[sub, pl.ds(start, band_rows), :] = shifted_part - image_next

    return pl.pallas_call(
        kernel,
        out_shape=[jax.ShapeDtypeStruct(shifted.shape, F32)] * 2,
        in_specs=[vmem()] * (1 + bands),
        out_specs=[vmem()] * 2,
        compiler_params=params(),
        name="finish",
    )(shifted, *noises)


def exchange(parts, bands):
    return [parts[0]] + [
        lax.ppermute(parts[k], "band", [(i, (i + k) % bands) for i in range(bands)])
        for k in range(1, bands)
    ]


def body(
    visibility,
    uv_positions,
    destinations,
    column_slots,
    image_cube,
    dual_cube,
    step_sizes,
    conv_first,
    conv_middle,
    conv_last,
):
    facets = lax.axis_size("facet")
    bands = lax.axis_size("band")
    subs, blocks = visibility.shape[:2]
    rows, width = image_cube.shape[1:]
    pairs = max(2, 2 * blocks // facets) // 2
    packed = pack_blocks(visibility, uv_positions, destinations, column_slots, facets, pairs)
    received = lax.all_to_all(packed, "facet", split_axis=0, concat_axis=0, tiled=True)
    weights = weight_matrices(conv_first, conv_middle, conv_last)
    shifted, edge_l, edge_r, *pieces = grid_and_step(
        received, image_cube, dual_cube, step_sizes, pairs, bands
    )
    from_left = lax.ppermute(edge_r, "facet", [(i, i + 1) for i in range(facets - 1)])
    from_right = lax.ppermute(edge_l, "facet", [(i + 1, i) for i in range(facets - 1)])
    edge = jnp.concatenate([from_left, from_right], axis=1)
    me = lax.axis_index("band")
    edge_parts = [
        lax.dynamic_index_in_dim(edge, (me + k) % bands, 0, keepdims=False) for k in range(bands)
    ]
    pieces = exchange(pieces, bands)
    edges = exchange(edge_parts, bands)
    noises = denoise(pieces, edges, *weights, subs, bands, rows // bands, width)
    return tuple(finish(shifted, exchange(noises, bands), bands))


def solution(mesh):
    return jax.shard_map(
        body,
        mesh=mesh,
        in_specs=(
            P("band", "facet", None, None),
            P("band", "facet", None, None),
            P("band", "facet", None),
            P("band", "facet"),
            P("band", None, "facet"),
            P("band", None, "facet"),
            P("band"),
            P(),
            P(),
            P(),
        ),
        out_specs=(P("band", None, "facet"), P("band", None, "facet")),
        check_vma=False,
    )
```

```python
import jax
import jax.numpy as jnp
from jax import lax
from jax.experimental import pallas as pl
from jax.experimental.pallas import tpu as pltpu
from jax.sharding import PartitionSpec as P

P_SIZE = 256
KW = 8
S = 64
HALF = P_SIZE // 2
CENTRE = (P_SIZE - KW + HALF) // 2
HALO = 4
PAD = 8
GROUP = 8
CH = 64
CHUNKS = 4
BF = jnp.bfloat16
F32 = jnp.float32


def params(mib=24):
    return pltpu.CompilerParams(vmem_limit_bytes=mib << 20)


def vmem():
    return pl.BlockSpec(memory_space=pltpu.VMEM)


def smem():
    return pl.BlockSpec(memory_space=pltpu.SMEM)


def pack_blocks(visibility, uv_positions, destinations, column_slots, facets, pairs):
    subs, blocks = visibility.shape[:2]
    vis_rows = subs * pairs * S
    pos_rows = -(-2 * subs * pairs // 16) * 16

    chunk = blocks // CHUNKS

    def kernel(
        dest_hbm, slot_hbm, vis_hbm, pos_hbm, out_ref,
        dest_ref, slot_ref, vis_ref, pos_ref, count_ref, place_ref, side_ref, sems,
    ):
        small = [
            pltpu.make_async_copy(dest_hbm, dest_ref, sems.at[CHUNKS]),
            pltpu.make_async_copy(slot_hbm, slot_ref, sems.at[CHUNKS + 1]),
            pltpu.make_async_copy(pos_hbm, pos_ref, sems.at[CHUNKS + 2]),
        ]
        large = [
            pltpu.make_async_copy(
                vis_hbm.at[:, pl.ds(c * chunk, chunk)], vis_ref.at[:, pl.ds(c * chunk, chunk)], sems.at[c]
            )
            for c in range(CHUNKS)
        ]
        for copy in small + large:
            copy.start()
        side_ref[...] = jnp.zeros(side_ref.shape, BF)
        place_ref[...] = jnp.zeros(place_ref.shape, F32)
        for n in range(subs * facets):
            count_ref[n] = 0
        for copy in small:
            copy.wait()

        def one(n, carry):
            for sub in range(subs):
                facet = dest_ref[sub, n]
                slot = slot_ref[sub, n]
                count = count_ref[sub * facets + facet]
                count_ref[sub * facets + facet] = count + 1
                pair = count // 2
                side = count - 2 * pair
                side_ref[side, facet, sub * pairs + pair] = vis_ref[sub, n]
                where = facet * pos_rows + sub * pairs + pair
                place = pos_ref[sub, n].astype(F32)
                shift = (slot * HALF - CENTRE).astype(F32)
                place_ref[side, pl.ds(where, 1), :] = place[0:1]
                place_ref[side, pl.ds(where + subs * pairs, 1), :] = place[1:2] + shift
            return carry

        for c in range(CHUNKS):
            large[c].wait()
            lax.fori_loop(c * chunk, (c + 1) * chunk, one, 0, unroll=4)
        for facet in range(facets):
            both = jnp.concatenate([side_ref[0, facet], side_ref[1, facet]], axis=2)
            out_ref[facet, :vis_rows, :] = both.reshape(vis_rows, 2 * S)
        both = jnp.concatenate([place_ref[0], place_ref[1]], axis=1).astype(BF)
        out_ref[:, vis_rows:, :] = both.reshape(facets, pos_rows, 2 * S)

    hbm = pl.BlockSpec(memory_space=pltpu.HBM)
    return pl.pallas_call(
        kernel,
        out_shape=jax.ShapeDtypeStruct((facets, vis_rows + pos_rows, 2 * S), BF),
        in_specs=[hbm] * 4,
        out_specs=vmem(),
        scratch_shapes=[
            pltpu.SMEM((subs, blocks), jnp.int32),
            pltpu.SMEM((subs, blocks), jnp.int32),
            pltpu.VMEM((subs, blocks, S, S), BF),
            pltpu.VMEM((subs, blocks, 2, S), jnp.int32),
            pltpu.SMEM((subs * facets,), jnp.int32),
            pltpu.VMEM((2, facets * pos_rows, S), F32),
            pltpu.VMEM((2, facets, subs * pairs, S, S), BF),
            pltpu.SemaphoreType.DMA((CHUNKS + 3,)),
        ],
        compiler_params=params(60),
        name="pack_blocks",
    )(destinations[..., 0], column_slots, visibility, uv_positions)


def taps(row, col):
    offset = col - row
    value = jnp.exp(-0.5 * ((offset.astype(F32) - (KW - 1) / 2.0) / (KW / 4.0)) ** 2)
    return jnp.where((offset >= 0) & (offset < KW), value, 0.0).astype(BF)


def contract_last(a, b):
    return lax.dot_general(a, b, (((1,), (1,)), ((), ())), preferred_element_type=F32)


def contract_first(a, b):
    return lax.dot_general(a, b, (((0,), (0,)), ((), ())), preferred_element_type=F32)


def dot(a, b):
    return jnp.dot(a, b, preferred_element_type=F32)


def grid_and_step(received, image, dual, steps, pairs, bands):
    facets = received.shape[0]
    subs, rows, width = image.shape
    vis_rows = subs * pairs * S
    per = 4
    sources = per // pairs
    band_rows = rows // bands
    piece = band_rows + 2 * HALO

    def kernel(step_ref, rec_ref, img_ref, dual_ref, shift_ref, edge_l, edge_r, *rest):
        piece_refs = rest[:bands]
        place_ref, acc_ref, den_ref = rest[bands:]
        place_ref[...] = rec_ref[:, vis_rows:, :].astype(F32)
        one = jnp.ones((), BF)
        none = jnp.zeros((), BF)
        lane = lax.broadcasted_iota(jnp.int32, (1, 2 * S), 1)
        left = jnp.where(lane < S, 1.0, 0.0).astype(BF)
        right = jnp.where(lane < S, 0.0, 1.0).astype(BF)
        zero = jnp.zeros((2 * S, 2 * S), BF)
        row_id = lax.broadcasted_iota(jnp.int32, (rows, 2 * S), 0).astype(F32).astype(BF)
        col_id = (lax.broadcasted_iota(jnp.int32, (width, 2 * S), 0) - CENTRE).astype(F32).astype(BF)

        for it in range(facets // sources):
            for sub in range(subs):
                first, second = [], []
                for q in range(per):
                    source = it * sources + q // pairs
                    at = sub * pairs + q % pairs
                    block = rec_ref[source, at * S : (at + 1) * S, :]
                    diag = jnp.concatenate([block * left, block * right], axis=0)
                    u_row = place_ref[source, at : at + 1, :].astype(BF)
                    v_row = place_ref[source, at + subs * pairs : at + subs * pairs + 1, :].astype(BF)
                    u_hot = jnp.where(row_id == u_row, one, none)
                    v_hot = jnp.where(col_id == v_row, one, none)
                    first.append((u_hot, diag))
                    second.append(v_hot)
                spread = []
                for q in range(0, per, 2):
                    hot = jnp.concatenate([first[q][0], first[q + 1][0]], axis=1)
                    block = jnp.concatenate(
                        [
                            jnp.concatenate([first[q][1], zero], axis=1),
                            jnp.concatenate([zero, first[q + 1][1]], axis=1),
                        ],
                        axis=0,
                    )
                    spread.append(dot(hot, block).astype(BF))
                term = contract_last(
                    jnp.concatenate(spread, axis=1), jnp.concatenate(second, axis=1)
                )
                acc_ref[sub] = term if it == 0 else acc_ref[sub] + term

        u_taps = taps(
            lax.broadcasted_iota(jnp.int32, (rows, rows), 1),
            lax.broadcasted_iota(jnp.int32, (rows, rows), 0),
        )
        v_taps = taps(
            lax.broadcasted_iota(jnp.int32, (width, width), 0),
            lax.broadcasted_iota(jnp.int32, (width, width), 1),
        )
        den_ref[...] = jnp.zeros(den_ref.shape, F32)
        me = lax.axis_index("band")
        for sub in range(subs):
            total = acc_ref[sub]
            high = total.astype(BF)
            low = (total - high.astype(F32)).astype(BF)
            half = dot(u_taps, high) + dot(u_taps, low)
            gradient = dot(half.astype(BF), v_taps)
            stepped = img_ref[sub] - step_ref[sub] * gradient
            shifted = stepped + dual_ref[sub]
            shift_ref[sub] = shifted
            den_ref[sub, HALO : HALO + rows, :] = shifted
        for k in range(bands):
            start = pl.multiple_of(lax.rem(me + k, bands) * band_rows, band_rows)
            piece_refs[k][...] = jnp.concatenate(
                [den_ref[sub, pl.ds(start, piece), :] for sub in range(subs)], axis=0
            ).astype(BF)
        pick_row = lax.broadcasted_iota(jnp.int32, (subs * HALO, HALF), 0)
        pick_lane = lax.broadcasted_iota(jnp.int32, (subs * HALO, HALF), 1)
        for k in range(bands):
            for ref, at, base in ((edge_l, 0, 0), (edge_r, width - HALF, HALF - HALO)):
                total = None
                for sub in range(subs):
                    pick = jnp.where(
                        (pick_row // HALO == sub) & (pick_lane == base + pick_row % HALO), 1.0, 0.0
                    ).astype(BF)
                    part = den_ref[sub, k * band_rows : k * band_rows + HALF, at : at + HALF].astype(BF)
                    term = contract_last(pick, part)
                    total = term if total is None else total + term
                ref[k] = total.astype(BF)

    edge = jax.ShapeDtypeStruct((bands, subs * HALO, HALF), BF)
    return pl.pallas_call(
        kernel,
        out_shape=[jax.ShapeDtypeStruct(image.shape, F32), edge, edge]
        + [jax.ShapeDtypeStruct((subs * piece, width), BF)] * bands,
        in_specs=[smem()] + [vmem()] * 3,
        out_specs=[vmem()] * (3 + bands),
        scratch_shapes=[
            pltpu.VMEM((facets, received.shape[1] - vis_rows, 2 * S), F32),
            pltpu.VMEM((subs, rows, width), F32),
            pltpu.VMEM((subs, (bands - 1) * band_rows + HALF, width), F32),
        ],
        compiler_params=params(),
        name="grid_and_step",
    )(steps, received, image, dual)


def weight_matrices(conv_first, conv_middle, conv_last):
    ci = conv_first.shape[1]
    co = conv_last.shape[0]
    first = conv_first.transpose(3, 2, 1, 0)
    middle = conv_middle.transpose(3, 2, 1, 0)
    last = conv_last[:, :, ::-1].transpose(3, 1, 2, 0).reshape(3, CH, 3 * co)
    ins = GROUP + 2
    outs = GROUP * co

    def kernel(first_ref, mid_ref, last_ref, one_ref, two_ref, three_ref):
        zero = jnp.zeros((ci, CH), F32)
        rows = []
        for t in range(3):
            for r in range(ins):
                parts = []
                for phase in range(2):
                    for k in range(GROUP // 2):
                        dy = r - 2 * k - phase
                        parts.append(first_ref[t, dy].astype(F32) if 0 <= dy < 3 else zero)
                rows.append(jnp.concatenate(parts, axis=1))
        one_ref[...] = jnp.concatenate(rows, axis=0).astype(BF)
        zero = jnp.zeros((CH, CH), BF)
        for t in range(3):
            for r in range(GROUP // 2 + 2):
                parts = [
                    mid_ref[t, r - k] if 0 <= r - k < 3 else zero for k in range(GROUP // 2)
                ]
                at = (t * (GROUP // 2 + 2) + r) * CH
                two_ref[at : at + CH, :] = jnp.concatenate(parts, axis=1)
        three_ref[...] = jnp.zeros(three_ref.shape, BF)
        lane = lax.broadcasted_iota(jnp.int32, (CH, 128), 1)
        keep = jnp.where(lane < outs, 1.0, 0.0)
        for r in range(ins):
            taps = []
            for t in range(3):
                base = jnp.concatenate(
                    [last_ref[t].astype(F32), jnp.zeros((CH, 128 - 3 * co), F32)], axis=1
                )
                taps.append(pltpu.roll(base, (r - 2) * co % 128, 1) * keep)
            block = jnp.concatenate([taps[0] + pltpu.roll(taps[1], outs, 1), taps[2]], axis=1)
            if r < GROUP:
                at = (r % 2 * (GROUP // 2) + r // 2) * CH
            else:
                at = GROUP * CH + (r - GROUP) * 2 * CH
            three_ref[at : at + CH, :] = block.astype(BF)

    return pl.pallas_call(
        kernel,
        out_shape=[
            jax.ShapeDtypeStruct((3 * ins * ci, GROUP * CH), BF),
            jax.ShapeDtypeStruct((3 * (GROUP // 2 + 2) * CH, GROUP // 2 * CH), BF),
            jax.ShapeDtypeStruct(((GROUP + 4) * CH, 256), BF),
        ],
        in_specs=[vmem()] * 3,
        out_specs=[vmem()] * 3,
        compiler_params=params(),
        cost_estimate=pl.CostEstimate(flops=1 << 20, bytes_accessed=1 << 20, transcendentals=0),
        name="weight_matrices",
    )(first, middle, last)


def denoise(pieces, edges, first, middle, last, subs, bands, band_rows, width):
    channels = subs * bands
    piece = band_rows + 2 * HALO
    groups = band_rows // GROUP + 1
    cols = width + 2 * PAD
    lanes = -(-cols // 128) * 128
    tall = -(-(cols + 2 * HALO) // 16) * 16
    in_rows = GROUP + 2
    facets = lax.axis_size("facet")

    def kernel(first_ref, mid_ref, last_ref, *rest):
        piece_refs = rest[:bands]
        edge_refs = rest[bands : 2 * bands]
        out_refs = rest[2 * bands : 3 * bands]
        x_ref, one_ref, two_ref, noise_ref = rest[3 * bands :]
        me = lax.axis_index("band")
        facet = lax.axis_index("facet")
        x_ref[:, piece * channels :, :] = jnp.zeros((lanes // 128, 2 * channels, 128), F32)
        one_ref[groups] = jnp.zeros(one_ref.shape[1:], BF)
        place_row = lax.broadcasted_iota(jnp.int32, (2 * subs * HALO, lanes), 0)
        place_lane = lax.broadcasted_iota(jnp.int32, (2 * subs * HALO, lanes), 1)
        side = place_row // (subs * HALO)
        spot = jnp.where(side == 0, PAD - HALO, PAD + width) + place_row % HALO
        for k in range(bands):
            band = lax.rem(me + bands - k, bands)
            for sub in range(subs):
                put = jnp.where(
                    (place_lane == spot) & (place_row // HALO % subs == sub), 1.0, 0.0
                ).astype(BF)
                halo = contract_first(edge_refs[k][...], put)[:piece]
                own = piece_refs[k][sub * piece : (sub + 1) * piece, :].astype(F32)
                own = jnp.concatenate([own, jnp.zeros((piece, lanes - width), F32)], axis=1)
                own = pltpu.roll(own, PAD, 1) + halo
                for part in range(lanes // 128):
                    x_ref[part, pl.ds(band * subs + sub, piece, stride=channels), :] = own[
                        :, part * 128 : (part + 1) * 128
                    ]

        col = lax.broadcasted_iota(jnp.int32, (1, lanes), 1) - PAD
        inside = ((col >= 0) | (facet > 0)) & ((col < width) | (facet < facets - 1))
        inside = jnp.where(inside, 1.0, 0.0)
        lane_id = lax.broadcasted_iota(jnp.int32, (1, GROUP * CH), 1)
        lane_row = lane_id // (GROUP // 2 * CH) + 2 * (lane_id // CH % (GROUP // 2))

        def layer_one(g):
            top = g * GROUP * channels
            x = jnp.concatenate(
                [x_ref[part, top : top + in_rows * channels, :] for part in range(lanes // 128)], axis=1
            )
            stack = jnp.concatenate(
                [pltpu.roll(x, 1, 1) * inside, x * inside, pltpu.roll(x, lanes - 1, 1) * inside], axis=0
            )
            stack = stack.astype(BF).T[:cols]
            hidden = dot(stack, first_ref[...])
            row = lane_row + (g * GROUP + 1 - HALO) + me * band_rows
            keep = jnp.where((row >= 0) & (row < band_rows * bands), 1.0, 0.0)
            one_ref[g, 0:cols, :] = (jnp.maximum(hidden, 0.0) * keep).astype(BF)

        block = GROUP // 2 * CH

        def layer_two(g):
            row = lane_row + (g * GROUP - 1) + me * band_rows
            keep = jnp.where((row >= 0) & (row < band_rows * bands), 1.0, 0.0)
            for phase in range(2):
                here = one_ref[g, :, phase * block : (phase + 1) * block]
                after = one_ref[g + 1, :, phase * block : phase * block + 2 * CH]
                parts = []
                for t in range(3):
                    parts += [here[2 * t : 2 * t + cols], after[2 * t : 2 * t + cols]]
                hidden = dot(jnp.concatenate(parts, axis=1), mid_ref[...])
                part = keep[:, phase * block : (phase + 1) * block]
                two_ref[g, :, phase * block : (phase + 1) * block] = (
                    jnp.maximum(hidden, 0.0) * part
                ).astype(BF)

        out_ch = channels * GROUP
        out_col = lax.broadcasted_iota(jnp.int32, (1, width), 1)
        has_left = jnp.where((out_col > 0) | (facet > 0), 1.0, 0.0)
        has_right = jnp.where((out_col < width - 1) | (facet < facets - 1), 1.0, 0.0)

        def layer_three(g):
            hidden = jnp.concatenate(
                [
                    two_ref[g],
                    two_ref[g + 1, :, 0 : 2 * CH],
                    two_ref[g + 1, :, block : block + 2 * CH],
                ],
                axis=1,
            )
            y = dot(hidden, last_ref[...]).T
            base = PAD - 2
            noise = (
                y[:out_ch, base - 1 : base - 1 + width] * has_left
                + y[out_ch : 2 * out_ch, base : base + width]
                + y[2 * out_ch : 3 * out_ch, base + 1 : base + 1 + width] * has_right
            )
            for part in range(width // 128):
                noise_ref[part, g * out_ch : (g + 1) * out_ch, :] = noise[
                    :, part * 128 : (part + 1) * 128
                ]

        for g in range(groups + 4):
            if g < groups:
                layer_one(g)
            if 0 <= g - 2 < groups:
                layer_two(g - 2)
            if 0 <= g - 4 < groups - 1:
                layer_three(g - 4)
        for k in range(bands):
            band = lax.rem(me + k, bands)
            for sub in range(subs):
                for part in range(width // 128):
                    out_refs[k][
                        sub * band_rows : (sub + 1) * band_rows, part * 128 : (part + 1) * 128
                    ] = noise_ref[
                        part, pl.ds(band * subs + sub, band_rows, stride=channels), :
                    ].astype(BF)

    return pl.pallas_call(
        kernel,
        out_shape=[jax.ShapeDtypeStruct((subs * band_rows, width), BF)] * bands,
        in_specs=[vmem()] * (3 + 2 * bands),
        out_specs=[vmem()] * bands,
        scratch_shapes=[
            pltpu.VMEM((lanes // 128, (groups * GROUP + 2) * channels, 128), F32),
            pltpu.VMEM((groups + 1, tall, GROUP * CH), BF),
            pltpu.VMEM((groups, cols, GROUP * CH), BF),
            pltpu.VMEM((width // 128, band_rows * channels, 128), F32),
        ],
        compiler_params=params(32),
        name="denoise",
    )(first, middle, last, *pieces, *edges)


def finish(shifted, noises, bands):
    subs, rows, width = shifted.shape
    band_rows = rows // bands

    def kernel(shift_ref, *rest):
        noise_refs = rest[:bands]
        img_ref, dual_ref = rest[bands:]
        me = lax.axis_index("band")
        for k in range(bands):
            start = pl.multiple_of(lax.rem(me + bands - k, bands) * band_rows, band_rows)
            for sub in range(subs):
                noise = noise_refs[k][sub * band_rows : (sub + 1) * band_rows, :].astype(F32)
                shifted_part = shift_ref[sub, pl.ds(start, band_rows), :]
                image_next = jnp.maximum(shifted_part - noise, 0.0)
                img_ref[sub, pl.ds(start, band_rows), :] = image_next
                dual_ref[sub, pl.ds(start, band_rows), :] = shifted_part - image_next

    return pl.pallas_call(
        kernel,
        out_shape=[jax.ShapeDtypeStruct(shifted.shape, F32)] * 2,
        in_specs=[vmem()] * (1 + bands),
        out_specs=[vmem()] * 2,
        compiler_params=params(),
        name="finish",
    )(shifted, *noises)


def exchange(parts, bands):
    return [parts[0]] + [
        lax.ppermute(parts[k], "band", [(i, (i + k) % bands) for i in range(bands)])
        for k in range(1, bands)
    ]


def body(
    visibility,
    uv_positions,
    destinations,
    column_slots,
    image_cube,
    dual_cube,
    step_sizes,
    conv_first,
    conv_middle,
    conv_last,
):
    facets = lax.axis_size("facet")
    bands = lax.axis_size("band")
    subs, blocks = visibility.shape[:2]
    rows, width = image_cube.shape[1:]
    pairs = max(2, 2 * blocks // facets) // 2
    packed = pack_blocks(visibility, uv_positions, destinations, column_slots, facets, pairs)
    received = lax.all_to_all(packed, "facet", split_axis=0, concat_axis=0, tiled=True)
    weights = weight_matrices(conv_first, conv_middle, conv_last)
    shifted, edge_l, edge_r, *pieces = grid_and_step(
        received, image_cube, dual_cube, step_sizes, pairs, bands
    )
    from_left = lax.ppermute(edge_r, "facet", [(i, i + 1) for i in range(facets - 1)])
    from_right = lax.ppermute(edge_l, "facet", [(i + 1, i) for i in range(facets - 1)])
    edge = jnp.concatenate([from_left, from_right], axis=1)
    me = lax.axis_index("band")
    edge_parts = [
        lax.dynamic_index_in_dim(edge, (me + k) % bands, 0, keepdims=False) for k in range(bands)
    ]
    pieces = exchange(pieces, bands)
    edges = exchange(edge_parts, bands)
    noises = denoise(pieces, edges, *weights, subs, bands, rows // bands, width)
    return tuple(finish(shifted, exchange(noises, bands), bands))


def solution(mesh):
    return jax.shard_map(
        body,
        mesh=mesh,
        in_specs=(
            P("band", "facet", None, None),
            P("band", "facet", None, None),
            P("band", "facet", None),
            P("band", "facet"),
            P("band", None, "facet"),
            P("band", None, "facet"),
            P("band"),
            P(),
            P(),
            P(),
        ),
        out_specs=(P("band", None, "facet"), P("band", None, "facet")),
        check_vma=False,
    )
```

```python
import jax
import jax.numpy as jnp
from jax import lax
from jax.experimental import pallas as pl
from jax.experimental.pallas import tpu as pltpu
from jax.sharding import PartitionSpec as P

P_SIZE = 256
KW = 8
S = 64
HALF = P_SIZE // 2
CENTRE = (P_SIZE - KW + HALF) // 2
HALO = 4
PAD = 8
GROUP = 8
CH = 64
CHUNKS = 4
BF = jnp.bfloat16
F32 = jnp.float32


def params(mib=24):
    return pltpu.CompilerParams(vmem_limit_bytes=mib << 20)


def vmem():
    return pl.BlockSpec(memory_space=pltpu.VMEM)


def smem():
    return pl.BlockSpec(memory_space=pltpu.SMEM)


def taps(row, col):
    offset = col - row
    value = jnp.exp(-0.5 * ((offset.astype(F32) - (KW - 1) / 2.0) / (KW / 4.0)) ** 2)
    return jnp.where((offset >= 0) & (offset < KW), value, 0.0).astype(BF)


def contract_last(a, b):
    return lax.dot_general(a, b, (((1,), (1,)), ((), ())), preferred_element_type=F32)


def contract_first(a, b):
    return lax.dot_general(a, b, (((0,), (0,)), ((), ())), preferred_element_type=F32)


def dot(a, b):
    return jnp.dot(a, b, preferred_element_type=F32)


def tap_matrix(size):
    shape = (size, size)
    return taps(lax.broadcasted_iota(jnp.int32, shape, 1), lax.broadcasted_iota(jnp.int32, shape, 0))


def pack_blocks(
    visibility, uv_positions, destinations, column_slots, image, dual, steps, facets, pairs
):
    rows, width = image.shape[1:]
    subs, blocks = visibility.shape[:2]
    vis_rows = subs * pairs * S
    pos_rows = -(-2 * subs * pairs // 16) * 16

    chunk = blocks // CHUNKS
    halo_rows = 2 * HALO * subs * (rows // 128)

    def kernel(
        dest_hbm, slot_hbm, vis_hbm, pos_hbm, img_hbm, dual_hbm, step_hbm, out_hbm,
        dest_ref, slot_ref, vis_ref, pos_ref, edge_ref, step_ref, count_ref, place_ref, side_ref,
        main_ref, halo_ref, sems,
    ):
        small = [
            pltpu.make_async_copy(dest_hbm, dest_ref, sems.at[CHUNKS]),
            pltpu.make_async_copy(slot_hbm, slot_ref, sems.at[CHUNKS + 1]),
            pltpu.make_async_copy(pos_hbm, pos_ref, sems.at[CHUNKS + 2]),
        ]
        large = [
            pltpu.make_async_copy(
                vis_hbm.at[:, pl.ds(c * chunk, chunk)], vis_ref.at[:, pl.ds(c * chunk, chunk)], sems.at[c]
            )
            for c in range(CHUNKS)
        ]
        edges = [
            pltpu.make_async_copy(step_hbm, step_ref, sems.at[CHUNKS + 3]),
        ] + [
            pltpu.make_async_copy(
                ref.at[:, :, pl.ds(at, 128)], edge_ref.at[n, side], sems.at[CHUNKS + 4 + 2 * n + side]
            )
            for n, ref in enumerate((img_hbm, dual_hbm))
            for side, at in enumerate((0, width - 128))
        ]
        for copy in small + large + edges:
            copy.start()
        side_ref[...] = jnp.zeros(side_ref.shape, BF)
        place_ref[...] = jnp.zeros(place_ref.shape, F32)
        for n in range(subs * facets):
            count_ref[n] = 0
        wide = facets * 4 * HALO
        cell_row = lax.broadcasted_iota(jnp.int32, (4 * HALO, 2 * S), 0)
        cell_lane = lax.broadcasted_iota(jnp.int32, (4 * HALO, 2 * S), 1)
        cell = cell_row % HALO + (width - KW - HALO + 1) * (cell_row // HALO % 2) - CENTRE
        cell = jnp.where(cell_lane // S == cell_row // (2 * HALO), cell, 2 * P_SIZE)
        cell = cell.astype(F32).astype(BF)
        lane = lax.broadcasted_iota(jnp.int32, (1, 4 * HALO), 1)
        mine = [
            jnp.where(lane // (2 * HALO) == block, 1.0, 0.0).astype(BF) for block in range(2)
        ]
        row_id = lax.broadcasted_iota(jnp.int32, (rows, 2 * S), 0).astype(F32).astype(BF)
        yes = jnp.ones((), BF)
        no = jnp.zeros((), BF)
        shape = (wide, facets * 2 * HALO)
        src = lax.broadcasted_iota(jnp.int32, shape, 0)
        dst = lax.broadcasted_iota(jnp.int32, shape, 1)
        halo_side = dst // HALO % 2
        meets = (src // (4 * HALO) == dst // (2 * HALO) + 2 * halo_side - 1) & (
            src // HALO % 2 == 1 - halo_side
        )
        offset = dst % HALO - src % HALO + (KW - 1) * (1 - halo_side)
        v_taps = jnp.where(meets, taps(0, offset).astype(F32), 0.0).astype(BF)
        u_taps = tap_matrix(rows)
        me = lax.axis_index("facet")
        shape = (128, facets * 2 * HALO)
        src = lax.broadcasted_iota(jnp.int32, shape, 0)
        dst = lax.broadcasted_iota(jnp.int32, shape, 1)
        halo_side = dst // HALO % 2
        pick = [
            jnp.where(
                (src == dst % HALO + (128 - HALO) * side)
                & (halo_side == 1 - side)
                & (dst // (2 * HALO) == me + 2 * side - 1),
                1.0,
                0.0,
            ).astype(BF)
            for side in range(2)
        ]
        for copy in small:
            copy.wait()

        def one(n, carry):
            for sub in range(subs):
                facet = dest_ref[sub, n]
                slot = slot_ref[sub, n]
                count = count_ref[sub * facets + facet]
                count_ref[sub * facets + facet] = count + 1
                pair = count // 2
                side = count - 2 * pair
                side_ref[side, facet, sub * pairs + pair] = vis_ref[sub, n]
                where = facet * pos_rows + sub * pairs + pair
                place = pos_ref[sub, n].astype(F32)
                shift = (slot * HALF - CENTRE).astype(F32)
                place_ref[side, pl.ds(where, 1), :] = place[0:1]
                place_ref[side, pl.ds(where + subs * pairs, 1), :] = place[1:2] + shift
            return carry

        for c in range(CHUNKS):
            large[c].wait()
            lax.fori_loop(c * chunk, (c + 1) * chunk, one, 0, unroll=4)
        for facet in range(facets):
            both = jnp.concatenate([side_ref[0, facet], side_ref[1, facet]], axis=2)
            main_ref[facet, :vis_rows, :] = both.reshape(vis_rows, 2 * S)
        both = jnp.concatenate([place_ref[0], place_ref[1]], axis=1)
        main_ref[:, vis_rows:, :] = both.astype(BF).reshape(facets, pos_rows, 2 * S)
        sent = [
            pltpu.make_async_copy(
                main_ref, out_hbm.at[:, pl.ds(0, vis_rows + pos_rows)], sems.at[CHUNKS + 8]
            ),
            pltpu.make_async_copy(
                halo_ref, out_hbm.at[:, pl.ds(vis_rows + pos_rows, halo_rows)], sems.at[CHUNKS + 9]
            ),
        ]
        sent[0].start()

        for copy in edges:
            copy.wait()
        halos = []
        for sub in range(subs):
            totals = []
            for facet in range(facets):
                hots, parts = [], []
                for pair in range(pairs):
                    at = sub * pairs + pair
                    where = facet * pos_rows + at
                    u_row = both[where : where + 1].astype(BF)
                    v_row = both[where + subs * pairs : where + subs * pairs + 1].astype(BF)
                    hots.append(jnp.where(row_id == u_row, yes, no))
                    hot = jnp.where(cell == v_row, yes, no)
                    found = contract_last(main_ref[facet, at * S : (at + 1) * S, :], hot).astype(BF)
                    parts += [found * mine[0], found * mine[1]]
                totals.append(dot(jnp.concatenate(hots, axis=1), jnp.concatenate(parts, axis=0)))
            total = jnp.concatenate(totals, axis=1)
            gradient = dot(dot(u_taps, total.astype(BF)).astype(BF), v_taps)
            halo = -step_ref[sub] * gradient
            for side in range(2):
                base = edge_ref[0, side, sub] + edge_ref[1, side, sub]
                halo += dot(base.astype(BF), pick[side])
            halos.append(halo.T.reshape(facets, 2 * HALO, rows))
        halo = jnp.concatenate(halos, axis=1).astype(BF)
        height = 2 * HALO * subs
        for part in range(rows // 128):
            halo_ref[:, part * height : (part + 1) * height, :] = halo[
                :, :, part * 128 : (part + 1) * 128
            ]
        sent[1].start()
        for copy in sent:
            copy.wait()

    hbm = pl.BlockSpec(memory_space=pltpu.HBM)
    return pl.pallas_call(
        kernel,
        out_shape=jax.ShapeDtypeStruct((facets, vis_rows + pos_rows + halo_rows, 2 * S), BF),
        in_specs=[hbm] * 7,
        out_specs=hbm,
        scratch_shapes=[
            pltpu.SMEM((subs, blocks), jnp.int32),
            pltpu.SMEM((subs, blocks), jnp.int32),
            pltpu.VMEM((subs, blocks, S, S), BF),
            pltpu.VMEM((subs, blocks, 2, S), jnp.int32),
            pltpu.VMEM((2, 2, subs, rows, 128), F32),
            pltpu.SMEM((subs,), F32),
            pltpu.SMEM((subs * facets,), jnp.int32),
            pltpu.VMEM((2, facets * pos_rows, S), F32),
            pltpu.VMEM((2, facets, subs * pairs, S, S), BF),
            pltpu.VMEM((facets, vis_rows + pos_rows, 2 * S), BF),
            pltpu.VMEM((facets, halo_rows, 2 * S), BF),
            pltpu.SemaphoreType.DMA((CHUNKS + 10,)),
        ],
        compiler_params=params(60),
        name="pack_blocks",
    )(destinations[..., 0], column_slots, visibility, uv_positions, image, dual, steps)


def grid_and_step(received, image, dual, steps, pairs, bands):
    facets = received.shape[0]
    subs, rows, width = image.shape
    vis_rows = subs * pairs * S
    per = 4
    sources = per // pairs
    band_rows = rows // bands
    piece = band_rows + 2 * HALO
    pos_rows = -(-2 * subs * pairs // 16) * 16
    height = 2 * HALO * subs

    def kernel(step_ref, rec_ref, img_ref, dual_ref, shift_ref, *rest):
        piece_refs = rest[:bands]
        place_ref, acc_ref, den_ref, halo_ref = rest[bands:]
        place_ref[...] = rec_ref[:, vis_rows : vis_rows + pos_rows, :].astype(F32)
        one = jnp.ones((), BF)
        none = jnp.zeros((), BF)
        lane = lax.broadcasted_iota(jnp.int32, (1, 2 * S), 1)
        left = jnp.where(lane < S, 1.0, 0.0).astype(BF)
        right = jnp.where(lane < S, 0.0, 1.0).astype(BF)
        zero = jnp.zeros((2 * S, 2 * S), BF)
        row_id = lax.broadcasted_iota(jnp.int32, (rows, 2 * S), 0).astype(F32).astype(BF)
        col_id = (lax.broadcasted_iota(jnp.int32, (width, 2 * S), 0) - CENTRE).astype(F32).astype(BF)

        for it in range(facets // sources):
            for sub in range(subs):
                first, second = [], []
                for q in range(per):
                    source = it * sources + q // pairs
                    at = sub * pairs + q % pairs
                    block = rec_ref[source, at * S : (at + 1) * S, :]
                    diag = jnp.concatenate([block * left, block * right], axis=0)
                    u_row = place_ref[source, at : at + 1, :].astype(BF)
                    v_row = place_ref[source, at + subs * pairs : at + subs * pairs + 1, :].astype(BF)
                    u_hot = jnp.where(row_id == u_row, one, none)
                    v_hot = jnp.where(col_id == v_row, one, none)
                    first.append((u_hot, diag))
                    second.append(v_hot)
                spread = []
                for q in range(0, per, 2):
                    hot = jnp.concatenate([first[q][0], first[q + 1][0]], axis=1)
                    block = jnp.concatenate(
                        [
                            jnp.concatenate([first[q][1], zero], axis=1),
                            jnp.concatenate([zero, first[q + 1][1]], axis=1),
                        ],
                        axis=0,
                    )
                    spread.append(dot(hot, block).astype(BF))
                term = contract_last(
                    jnp.concatenate(spread, axis=1), jnp.concatenate(second, axis=1)
                )
                acc_ref[sub] = term if it == 0 else acc_ref[sub] + term

        u_taps = tap_matrix(rows)
        v_taps = taps(
            lax.broadcasted_iota(jnp.int32, (width, width), 0),
            lax.broadcasted_iota(jnp.int32, (width, width), 1),
        )
        den_ref[...] = jnp.zeros(den_ref.shape, F32)
        me = lax.axis_index("band")
        for sub in range(subs):
            total = acc_ref[sub]
            high = total.astype(BF)
            low = (total - high.astype(F32)).astype(BF)
            half = dot(u_taps, high) + dot(u_taps, low)
            gradient = dot(half.astype(BF), v_taps)
            stepped = img_ref[sub] - step_ref[sub] * gradient
            shifted = stepped + dual_ref[sub]
            shift_ref[sub] = shifted
            den_ref[sub, HALO : HALO + rows, :] = shifted
        halo = jnp.sum(rec_ref[:, vis_rows + pos_rows :, :].astype(F32), axis=0)
        parts = [halo[n * height : (n + 1) * height] for n in range(rows // 128)]
        halo = jnp.concatenate(parts + [jnp.zeros((height, 128), F32)], axis=1)
        steps_in = 128 // band_rows
        for n in range(steps_in):
            shift = (HALO - n * band_rows) % (rows + 128)
            moved = pltpu.roll(halo, shift, 1)
            for tile in range(bands // steps_in):
                halo_ref[tile * steps_in + n] = moved[:, tile * 128 : (tile + 1) * 128]
        blank = jnp.zeros((height, width - 128), F32)
        for k in range(bands):
            band = lax.rem(me + k, bands)
            start = pl.multiple_of(band * band_rows, band_rows)
            piece_refs[k][...] = jnp.concatenate(
                [den_ref[sub, pl.ds(start, piece), :] for sub in range(subs)]
                + [jnp.concatenate([halo_ref[band], blank], axis=1)],
                axis=0,
            ).astype(BF)

    return pl.pallas_call(
        kernel,
        out_shape=[jax.ShapeDtypeStruct(image.shape, F32)]
        + [jax.ShapeDtypeStruct((subs * piece + height, width), BF)] * bands,
        in_specs=[smem()] + [vmem()] * 3,
        out_specs=[vmem()] * (1 + bands),
        scratch_shapes=[
            pltpu.VMEM((facets, pos_rows, 2 * S), F32),
            pltpu.VMEM((subs, rows, width), F32),
            pltpu.VMEM((subs, rows + 2 * HALO, width), F32),
            pltpu.VMEM((bands, height, 128), F32),
        ],
        compiler_params=params(),
        name="grid_and_step",
    )(steps, received, image, dual)


def weight_matrices(conv_first, conv_middle, conv_last):
    ci = conv_first.shape[1]
    co = conv_last.shape[0]
    first = conv_first.transpose(3, 2, 1, 0)
    middle = conv_middle.transpose(3, 2, 1, 0)
    last = conv_last[:, :, ::-1].transpose(3, 1, 2, 0).reshape(3, CH, 3 * co)
    ins = GROUP + 2
    outs = GROUP * co

    def kernel(first_ref, mid_ref, last_ref, one_ref, two_ref, three_ref):
        zero = jnp.zeros((ci, CH), F32)
        rows = []
        for t in range(3):
            for r in range(ins):
                parts = []
                for phase in range(2):
                    for k in range(GROUP // 2):
                        dy = r - 2 * k - phase
                        parts.append(first_ref[t, dy].astype(F32) if 0 <= dy < 3 else zero)
                rows.append(jnp.concatenate(parts, axis=1))
        one_ref[...] = jnp.concatenate(rows, axis=0).astype(BF)
        zero = jnp.zeros((CH, CH), BF)
        for t in range(3):
            for r in range(GROUP // 2 + 2):
                parts = [
                    mid_ref[t, r - k] if 0 <= r - k < 3 else zero for k in range(GROUP // 2)
                ]
                at = (t * (GROUP // 2 + 2) + r) * CH
                two_ref[at : at + CH, :] = jnp.concatenate(parts, axis=1)
        three_ref[...] = jnp.zeros(three_ref.shape, BF)
        lane = lax.broadcasted_iota(jnp.int32, (CH, 128), 1)
        keep = jnp.where(lane < outs, 1.0, 0.0)
        for r in range(ins):
            taps = []
            for t in range(3):
                base = jnp.concatenate(
                    [last_ref[t].astype(F32), jnp.zeros((CH, 128 - 3 * co), F32)], axis=1
                )
                taps.append(pltpu.roll(base, (r - 2) * co % 128, 1) * keep)
            block = jnp.concatenate([taps[0] + pltpu.roll(taps[1], outs, 1), taps[2]], axis=1)
            if r < GROUP:
                at = (r % 2 * (GROUP // 2) + r // 2) * CH
            else:
                at = GROUP * CH + (r - GROUP) * 2 * CH
            three_ref[at : at + CH, :] = block.astype(BF)

    return pl.pallas_call(
        kernel,
        out_shape=[
            jax.ShapeDtypeStruct((3 * ins * ci, GROUP * CH), BF),
            jax.ShapeDtypeStruct((3 * (GROUP // 2 + 2) * CH, GROUP // 2 * CH), BF),
            jax.ShapeDtypeStruct(((GROUP + 4) * CH, 256), BF),
        ],
        in_specs=[vmem()] * 3,
        out_specs=[vmem()] * 3,
        compiler_params=params(),
        cost_estimate=pl.CostEstimate(flops=1 << 20, bytes_accessed=1 << 20, transcendentals=0),
        name="weight_matrices",
    )(first, middle, last)


def denoise(pieces, first, middle, last, subs, bands, band_rows, width):
    channels = subs * bands
    piece = band_rows + 2 * HALO
    groups = band_rows // GROUP + 1
    cols = width + 2 * PAD
    lanes = -(-cols // 128) * 128
    tall = -(-(cols + 2 * HALO) // 16) * 16
    in_rows = GROUP + 2
    facets = lax.axis_size("facet")

    def kernel(first_ref, mid_ref, last_ref, *rest):
        piece_refs = rest[:bands]
        out_refs = rest[bands : 2 * bands]
        x_ref, one_ref, two_ref, noise_ref = rest[2 * bands :]
        me = lax.axis_index("band")
        facet = lax.axis_index("facet")
        x_ref[:, piece * channels :, :] = jnp.zeros((lanes // 128, 2 * channels, 128), F32)
        one_ref[groups] = jnp.zeros(one_ref.shape[1:], BF)
        place_row = lax.broadcasted_iota(jnp.int32, (2 * subs * HALO, lanes), 0)
        place_lane = lax.broadcasted_iota(jnp.int32, (2 * subs * HALO, lanes), 1)
        side = place_row // HALO % 2
        spot = jnp.where(side == 0, PAD - HALO, PAD + width) + place_row % HALO
        for k in range(bands):
            band = lax.rem(me + bands - k, bands)
            for sub in range(subs):
                put = jnp.where(
                    (place_lane == spot) & (place_row // (2 * HALO) == sub), 1.0, 0.0
                ).astype(BF)
                halo = contract_first(piece_refs[k][subs * piece :, 0:128], put)[:piece]
                own = piece_refs[k][sub * piece : (sub + 1) * piece, :].astype(F32)
                own = jnp.concatenate([own, jnp.zeros((piece, lanes - width), F32)], axis=1)
                own = pltpu.roll(own, PAD, 1) + halo
                for part in range(lanes // 128):
                    x_ref[part, pl.ds(band * subs + sub, piece, stride=channels), :] = own[
                        :, part * 128 : (part + 1) * 128
                    ]

        col = lax.broadcasted_iota(jnp.int32, (1, lanes), 1) - PAD
        inside = ((col >= 0) | (facet > 0)) & ((col < width) | (facet < facets - 1))
        inside = jnp.where(inside, 1.0, 0.0)
        lane_id = lax.broadcasted_iota(jnp.int32, (1, GROUP * CH), 1)
        lane_row = lane_id // (GROUP // 2 * CH) + 2 * (lane_id // CH % (GROUP // 2))

        def layer_one(g):
            top = g * GROUP * channels
            x = jnp.concatenate(
                [x_ref[part, top : top + in_rows * channels, :] for part in range(lanes // 128)], axis=1
            )
            stack = jnp.concatenate(
                [pltpu.roll(x, 1, 1) * inside, x * inside, pltpu.roll(x, lanes - 1, 1) * inside], axis=0
            )
            stack = stack.astype(BF).T[:cols]
            hidden = dot(stack, first_ref[...])
            row = lane_row + (g * GROUP + 1 - HALO) + me * band_rows
            keep = jnp.where((row >= 0) & (row < band_rows * bands), 1.0, 0.0)
            one_ref[g, 0:cols, :] = (jnp.maximum(hidden, 0.0) * keep).astype(BF)

        block = GROUP // 2 * CH

        def layer_two(g):
            row = lane_row + (g * GROUP - 1) + me * band_rows
            keep = jnp.where((row >= 0) & (row < band_rows * bands), 1.0, 0.0)
            for phase in range(2):
                here = one_ref[g, :, phase * block : (phase + 1) * block]
                after = one_ref[g + 1, :, phase * block : phase * block + 2 * CH]
                parts = []
                for t in range(3):
                    parts += [here[2 * t : 2 * t + cols], after[2 * t : 2 * t + cols]]
                hidden = dot(jnp.concatenate(parts, axis=1), mid_ref[...])
                part = keep[:, phase * block : (phase + 1) * block]
                two_ref[g, :, phase * block : (phase + 1) * block] = (
                    jnp.maximum(hidden, 0.0) * part
                ).astype(BF)

        out_ch = channels * GROUP
        out_col = lax.broadcasted_iota(jnp.int32, (1, width), 1)
        has_left = jnp.where((out_col > 0) | (facet > 0), 1.0, 0.0)
        has_right = jnp.where((out_col < width - 1) | (facet < facets - 1), 1.0, 0.0)

        def layer_three(g):
            hidden = jnp.concatenate(
                [
                    two_ref[g],
                    two_ref[g + 1, :, 0 : 2 * CH],
                    two_ref[g + 1, :, block : block + 2 * CH],
                ],
                axis=1,
            )
            y = dot(hidden, last_ref[...]).T
            base = PAD - 2
            noise = (
                y[:out_ch, base - 1 : base - 1 + width] * has_left
                + y[out_ch : 2 * out_ch, base : base + width]
                + y[2 * out_ch : 3 * out_ch, base + 1 : base + 1 + width] * has_right
            )
            for part in range(width // 128):
                noise_ref[part, g * out_ch : (g + 1) * out_ch, :] = noise[
                    :, part * 128 : (part + 1) * 128
                ]

        for g in range(groups + 4):
            if g < groups:
                layer_one(g)
            if 0 <= g - 2 < groups:
                layer_two(g - 2)
            if 0 <= g - 4 < groups - 1:
                layer_three(g - 4)
        for k in range(bands):
            band = lax.rem(me + k, bands)
            for sub in range(subs):
                for part in range(width // 128):
                    out_refs[k][
                        sub * band_rows : (sub + 1) * band_rows, part * 128 : (part + 1) * 128
                    ] = noise_ref[
                        part, pl.ds(band * subs + sub, band_rows, stride=channels), :
                    ].astype(BF)

    return pl.pallas_call(
        kernel,
        out_shape=[jax.ShapeDtypeStruct((subs * band_rows, width), BF)] * bands,
        in_specs=[vmem()] * (3 + bands),
        out_specs=[vmem()] * bands,
        scratch_shapes=[
            pltpu.VMEM((lanes // 128, (groups * GROUP + 2) * channels, 128), F32),
            pltpu.VMEM((groups + 1, tall, GROUP * CH), BF),
            pltpu.VMEM((groups, cols, GROUP * CH), BF),
            pltpu.VMEM((width // 128, band_rows * channels, 128), F32),
        ],
        compiler_params=params(32),
        name="denoise",
    )(first, middle, last, *pieces)


def finish(shifted, noises, bands):
    subs, rows, width = shifted.shape
    band_rows = rows // bands

    def kernel(shift_ref, *rest):
        noise_refs = rest[:bands]
        img_ref, dual_ref = rest[bands:]
        me = lax.axis_index("band")
        for k in range(bands):
            start = pl.multiple_of(lax.rem(me + bands - k, bands) * band_rows, band_rows)
            for sub in range(subs):
                noise = noise_refs[k][sub * band_rows : (sub + 1) * band_rows, :].astype(F32)
                shifted_part = shift_ref[sub, pl.ds(start, band_rows), :]
                image_next = jnp.maximum(shifted_part - noise, 0.0)
                img_ref[sub, pl.ds(start, band_rows), :] = image_next
                dual_ref[sub, pl.ds(start, band_rows), :] = shifted_part - image_next

    return pl.pallas_call(
        kernel,
        out_shape=[jax.ShapeDtypeStruct(shifted.shape, F32)] * 2,
        in_specs=[vmem()] * (1 + bands),
        out_specs=[vmem()] * 2,
        compiler_params=params(),
        name="finish",
    )(shifted, *noises)


def exchange(parts, bands):
    return [parts[0]] + [
        lax.ppermute(parts[k], "band", [(i, (i + k) % bands) for i in range(bands)])
        for k in range(1, bands)
    ]


def body(
    visibility,
    uv_positions,
    destinations,
    column_slots,
    image_cube,
    dual_cube,
    step_sizes,
    conv_first,
    conv_middle,
    conv_last,
):
    facets = lax.axis_size("facet")
    bands = lax.axis_size("band")
    subs, blocks = visibility.shape[:2]
    rows, width = image_cube.shape[1:]
    pairs = max(2, 2 * blocks // facets) // 2
    packed = pack_blocks(
        visibility,
        uv_positions,
        destinations,
        column_slots,
        image_cube,
        dual_cube,
        step_sizes,
        facets,
        pairs,
    )
    received = lax.all_to_all(packed, "facet", split_axis=0, concat_axis=0, tiled=True)
    weights = weight_matrices(conv_first, conv_middle, conv_last)
    shifted, *pieces = grid_and_step(received, image_cube, dual_cube, step_sizes, pairs, bands)
    pieces = exchange(pieces, bands)
    noises = denoise(pieces, *weights, subs, bands, rows // bands, width)
    return tuple(finish(shifted, exchange(noises, bands), bands))


def solution(mesh):
    return jax.shard_map(
        body,
        mesh=mesh,
        in_specs=(
            P("band", "facet", None, None),
            P("band", "facet", None, None),
            P("band", "facet", None),
            P("band", "facet"),
            P("band", None, "facet"),
            P("band", None, "facet"),
            P("band"),
            P(),
            P(),
            P(),
        ),
        out_specs=(P("band", None, "facet"), P("band", None, "facet")),
        check_vma=False,
    )
```

```python
import jax
import jax.numpy as jnp
from jax import lax
from jax.experimental import pallas as pl
from jax.experimental.pallas import tpu as pltpu
from jax.sharding import PartitionSpec as P

P_SIZE = 256
KW = 8
S = 64
HALF = P_SIZE // 2
CENTRE = (P_SIZE - KW + HALF) // 2
HALO = 4
PAD = 8
GROUP = 8
CH = 64
CHUNKS = 4
DEPTH = 2
BF = jnp.bfloat16
F32 = jnp.float32


def params(mib=24):
    return pltpu.CompilerParams(vmem_limit_bytes=mib << 20)


def vmem():
    return pl.BlockSpec(memory_space=pltpu.VMEM)


def smem():
    return pl.BlockSpec(memory_space=pltpu.SMEM)


def taps(row, col):
    offset = col - row
    value = jnp.exp(-0.5 * ((offset.astype(F32) - (KW - 1) / 2.0) / (KW / 4.0)) ** 2)
    return jnp.where((offset >= 0) & (offset < KW), value, 0.0).astype(BF)


def contract_last(a, b):
    return lax.dot_general(a, b, (((1,), (1,)), ((), ())), preferred_element_type=F32)


def contract_first(a, b):
    return lax.dot_general(a, b, (((0,), (0,)), ((), ())), preferred_element_type=F32)


def dot(a, b):
    return jnp.dot(a, b, preferred_element_type=F32)


def tap_matrix(size):
    shape = (size, size)
    return taps(lax.broadcasted_iota(jnp.int32, shape, 1), lax.broadcasted_iota(jnp.int32, shape, 0))


def pack_blocks(
    visibility, uv_positions, destinations, column_slots, image, dual, steps, facets, pairs
):
    rows, width = image.shape[1:]
    subs, blocks = visibility.shape[:2]
    vis_rows = subs * pairs * S
    pos_rows = -(-2 * subs * pairs // 16) * 16

    chunk = blocks // CHUNKS
    halo_rows = 2 * HALO * subs * (rows // 128)

    def kernel(
        dest_hbm, slot_hbm, vis_hbm, pos_hbm, img_hbm, dual_hbm, step_hbm, out_hbm,
        dest_ref, slot_ref, vis_ref, pos_ref, edge_ref, step_ref, count_ref, place_ref, side_ref,
        main_ref, halo_ref, sems,
    ):
        small = [
            pltpu.make_async_copy(dest_hbm, dest_ref, sems.at[CHUNKS]),
            pltpu.make_async_copy(slot_hbm, slot_ref, sems.at[CHUNKS + 1]),
            pltpu.make_async_copy(pos_hbm, pos_ref, sems.at[CHUNKS + 2]),
        ]
        large = [
            pltpu.make_async_copy(
                vis_hbm.at[:, pl.ds(c * chunk, chunk)], vis_ref.at[:, pl.ds(c * chunk, chunk)], sems.at[c]
            )
            for c in range(CHUNKS)
        ]
        edges = [
            pltpu.make_async_copy(step_hbm, step_ref, sems.at[CHUNKS + 3]),
        ] + [
            pltpu.make_async_copy(
                ref.at[:, :, pl.ds(at, 128)], edge_ref.at[n, side], sems.at[CHUNKS + 4 + 2 * n + side]
            )
            for n, ref in enumerate((img_hbm, dual_hbm))
            for side, at in enumerate((0, width - 128))
        ]
        for copy in small + large + edges:
            copy.start()
        side_ref[...] = jnp.zeros(side_ref.shape, BF)
        place_ref[...] = jnp.zeros(place_ref.shape, F32)
        for n in range(subs * facets):
            count_ref[n] = 0
        wide = facets * 4 * HALO
        cell_row = lax.broadcasted_iota(jnp.int32, (4 * HALO, 2 * S), 0)
        cell_lane = lax.broadcasted_iota(jnp.int32, (4 * HALO, 2 * S), 1)
        cell = cell_row % HALO + (width - KW - HALO + 1) * (cell_row // HALO % 2) - CENTRE
        cell = jnp.where(cell_lane // S == cell_row // (2 * HALO), cell, 2 * P_SIZE)
        cell = cell.astype(F32).astype(BF)
        lane = lax.broadcasted_iota(jnp.int32, (1, wide), 1)
        mine = [
            jnp.where(lane // (2 * HALO) % 2 == block, 1.0, 0.0).astype(BF) for block in range(2)
        ]
        row_id = lax.broadcasted_iota(jnp.int32, (rows, 2 * S), 0).astype(F32).astype(BF)
        yes = jnp.ones((), BF)
        no = jnp.zeros((), BF)
        shape = (wide, facets * 2 * HALO)
        src = lax.broadcasted_iota(jnp.int32, shape, 0)
        dst = lax.broadcasted_iota(jnp.int32, shape, 1)
        halo_side = dst // HALO % 2
        meets = (src // (4 * HALO) == dst // (2 * HALO) + 2 * halo_side - 1) & (
            src // HALO % 2 == 1 - halo_side
        )
        offset = dst % HALO - src % HALO + (KW - 1) * (1 - halo_side)
        v_taps = jnp.where(meets, taps(0, offset).astype(F32), 0.0).astype(BF)
        u_taps = tap_matrix(rows)
        me = lax.axis_index("facet")
        shape = (128, facets * 2 * HALO)
        src = lax.broadcasted_iota(jnp.int32, shape, 0)
        dst = lax.broadcasted_iota(jnp.int32, shape, 1)
        halo_side = dst // HALO % 2
        pick = [
            jnp.where(
                (src == dst % HALO + (128 - HALO) * side)
                & (halo_side == 1 - side)
                & (dst // (2 * HALO) == me + 2 * side - 1),
                1.0,
                0.0,
            ).astype(BF)
            for side in range(2)
        ]
        for copy in small:
            copy.wait()

        def one(n, carry):
            for sub in range(subs):
                facet = dest_ref[sub, n]
                slot = slot_ref[sub, n]
                count = count_ref[sub * facets + facet]
                count_ref[sub * facets + facet] = count + 1
                pair = count // 2
                side = count - 2 * pair
                side_ref[side, facet, sub * pairs + pair] = vis_ref[sub, n]
                where = facet * pos_rows + sub * pairs + pair
                place = pos_ref[sub, n].astype(F32)
                shift = (slot * HALF - CENTRE).astype(F32)
                place_ref[side, pl.ds(where, 1), :] = place[0:1]
                place_ref[side, pl.ds(where + subs * pairs, 1), :] = place[1:2] + shift
            return carry

        for c in range(CHUNKS):
            large[c].wait()
            lax.fori_loop(c * chunk, (c + 1) * chunk, one, 0, unroll=4)
        for facet in range(facets):
            both = jnp.concatenate([side_ref[0, facet], side_ref[1, facet]], axis=2)
            main_ref[facet, :vis_rows, :] = both.reshape(vis_rows, 2 * S)
        both = jnp.concatenate([place_ref[0], place_ref[1]], axis=1)
        main_ref[:, vis_rows:, :] = both.astype(BF).reshape(facets, pos_rows, 2 * S)
        sent = [
            pltpu.make_async_copy(
                main_ref, out_hbm.at[:, pl.ds(0, vis_rows + pos_rows)], sems.at[CHUNKS + 8]
            ),
            pltpu.make_async_copy(
                halo_ref, out_hbm.at[:, pl.ds(vis_rows + pos_rows, halo_rows)], sems.at[CHUNKS + 9]
            ),
        ]
        sent[0].start()

        for copy in edges:
            copy.wait()
        halos = []
        for sub in range(subs):
            hots, parts = [], []
            for facet in range(facets):
                for pair in range(pairs):
                    at = sub * pairs + pair
                    where = facet * pos_rows + at
                    u_row = both[where : where + 1].astype(BF)
                    v_row = both[where + subs * pairs : where + subs * pairs + 1].astype(BF)
                    hots.append(jnp.where(row_id == u_row, yes, no))
                    hot = jnp.where(cell == v_row, yes, no)
                    found = contract_last(main_ref[facet, at * S : (at + 1) * S, :], hot)
                    left, right = facet * 4 * HALO, (facets - facet - 1) * 4 * HALO
                    row = [jnp.zeros((S, left), F32)] if left else []
                    row += [found]
                    row += [jnp.zeros((S, right), F32)] if right else []
                    found = jnp.concatenate(row, axis=1).astype(BF)
                    parts += [found * mine[0], found * mine[1]]
            total = dot(jnp.concatenate(hots, axis=1), jnp.concatenate(parts, axis=0))
            gradient = dot(dot(u_taps, total.astype(BF)).astype(BF), v_taps)
            halo = -step_ref[sub] * gradient
            for side in range(2):
                base = edge_ref[0, side, sub] + edge_ref[1, side, sub]
                halo += dot(base.astype(BF), pick[side])
            halos.append(halo.T.reshape(facets, 2 * HALO, rows))
        halo = jnp.concatenate(halos, axis=1).astype(BF)
        height = 2 * HALO * subs
        for part in range(rows // 128):
            halo_ref[:, part * height : (part + 1) * height, :] = halo[
                :, :, part * 128 : (part + 1) * 128
            ]
        sent[1].start()
        for copy in sent:
            copy.wait()

    hbm = pl.BlockSpec(memory_space=pltpu.HBM)
    return pl.pallas_call(
        kernel,
        out_shape=jax.ShapeDtypeStruct((facets, vis_rows + pos_rows + halo_rows, 2 * S), BF),
        in_specs=[hbm] * 7,
        out_specs=hbm,
        scratch_shapes=[
            pltpu.SMEM((subs, blocks), jnp.int32),
            pltpu.SMEM((subs, blocks), jnp.int32),
            pltpu.VMEM((subs, blocks, S, S), BF),
            pltpu.VMEM((subs, blocks, 2, S), jnp.int32),
            pltpu.VMEM((2, 2, subs, rows, 128), F32),
            pltpu.SMEM((subs,), F32),
            pltpu.SMEM((subs * facets,), jnp.int32),
            pltpu.VMEM((2, facets * pos_rows, S), F32),
            pltpu.VMEM((2, facets, subs * pairs, S, S), BF),
            pltpu.VMEM((facets, vis_rows + pos_rows, 2 * S), BF),
            pltpu.VMEM((facets, halo_rows, 2 * S), BF),
            pltpu.SemaphoreType.DMA((CHUNKS + 10,)),
        ],
        compiler_params=params(60),
        name="pack_blocks",
    )(destinations[..., 0], column_slots, visibility, uv_positions, image, dual, steps)


def grid_and_step(received, image, dual, steps, pairs, bands):
    facets = received.shape[0]
    subs, rows, width = image.shape
    vis_rows = subs * pairs * S
    per = 4
    sources = per // pairs
    band_rows = rows // bands
    piece = band_rows + 2 * HALO
    pos_rows = -(-2 * subs * pairs // 16) * 16
    height = 2 * HALO * subs

    def kernel(step_ref, rec_ref, img_ref, dual_ref, shift_ref, *rest):
        piece_refs = rest[:bands]
        place_ref, acc_ref, den_ref, halo_ref = rest[bands:]
        place_ref[...] = rec_ref[:, vis_rows : vis_rows + pos_rows, :].astype(F32)
        one = jnp.ones((), BF)
        none = jnp.zeros((), BF)
        lane = lax.broadcasted_iota(jnp.int32, (1, 2 * S), 1)
        left = jnp.where(lane < S, 1.0, 0.0).astype(BF)
        right = jnp.where(lane < S, 0.0, 1.0).astype(BF)
        zero = jnp.zeros((2 * S, 2 * S), BF)
        row_id = lax.broadcasted_iota(jnp.int32, (rows, 2 * S), 0).astype(F32).astype(BF)
        col_id = (lax.broadcasted_iota(jnp.int32, (width, 2 * S), 0) - CENTRE).astype(F32).astype(BF)

        spreads = [[] for _ in range(subs)]
        hots = [[] for _ in range(subs)]
        for it in range(facets // sources):
            for sub in range(subs):
                first, second = [], []
                for q in range(per):
                    source = it * sources + q // pairs
                    at = sub * pairs + q % pairs
                    block = rec_ref[source, at * S : (at + 1) * S, :]
                    diag = jnp.concatenate([block * left, block * right], axis=0)
                    u_row = place_ref[source, at : at + 1, :].astype(BF)
                    v_row = place_ref[source, at + subs * pairs : at + subs * pairs + 1, :].astype(BF)
                    u_hot = jnp.where(row_id == u_row, one, none)
                    v_hot = jnp.where(col_id == v_row, one, none)
                    first.append((u_hot, diag))
                    second.append(v_hot)
                spread = []
                for q in range(0, per, 2):
                    hot = jnp.concatenate([first[q][0], first[q + 1][0]], axis=1)
                    block = jnp.concatenate(
                        [
                            jnp.concatenate([first[q][1], zero], axis=1),
                            jnp.concatenate([zero, first[q + 1][1]], axis=1),
                        ],
                        axis=0,
                    )
                    spread.append(dot(hot, block).astype(BF))
                spreads[sub] += spread
                hots[sub] += second
                if it % DEPTH == DEPTH - 1:
                    term = contract_last(
                        jnp.concatenate(spreads[sub], axis=1), jnp.concatenate(hots[sub], axis=1)
                    )
                    acc_ref[sub] = term if it < DEPTH else acc_ref[sub] + term
                    spreads[sub], hots[sub] = [], []

        u_taps = tap_matrix(rows)
        v_taps = taps(
            lax.broadcasted_iota(jnp.int32, (width, width), 0),
            lax.broadcasted_iota(jnp.int32, (width, width), 1),
        )
        den_ref[...] = jnp.zeros(den_ref.shape, F32)
        me = lax.axis_index("band")
        for sub in range(subs):
            total = acc_ref[sub]
            high = total.astype(BF)
            low = (total - high.astype(F32)).astype(BF)
            half = dot(u_taps, high) + dot(u_taps, low)
            gradient = dot(half.astype(BF), v_taps)
            stepped = img_ref[sub] - step_ref[sub] * gradient
            shifted = stepped + dual_ref[sub]
            shift_ref[sub] = shifted
            den_ref[sub, HALO : HALO + rows, :] = shifted
        halo = jnp.sum(rec_ref[:, vis_rows + pos_rows :, :].astype(F32), axis=0)
        parts = [halo[n * height : (n + 1) * height] for n in range(rows // 128)]
        halo = jnp.concatenate(parts + [jnp.zeros((height, 128), F32)], axis=1)
        steps_in = 128 // band_rows
        for n in range(steps_in):
            shift = (HALO - n * band_rows) % (rows + 128)
            moved = pltpu.roll(halo, shift, 1)
            for tile in range(bands // steps_in):
                halo_ref[tile * steps_in + n] = moved[:, tile * 128 : (tile + 1) * 128]
        blank = jnp.zeros((height, width - 128), F32)
        for k in range(bands):
            band = lax.rem(me + k, bands)
            start = pl.multiple_of(band * band_rows, band_rows)
            piece_refs[k][...] = jnp.concatenate(
                [den_ref[sub, pl.ds(start, piece), :] for sub in range(subs)]
                + [jnp.concatenate([halo_ref[band], blank], axis=1)],
                axis=0,
            ).astype(BF)

    return pl.pallas_call(
        kernel,
        out_shape=[jax.ShapeDtypeStruct(image.shape, F32)]
        + [jax.ShapeDtypeStruct((subs * piece + height, width), BF)] * bands,
        in_specs=[smem()] + [vmem()] * 3,
        out_specs=[vmem()] * (1 + bands),
        scratch_shapes=[
            pltpu.VMEM((facets, pos_rows, 2 * S), F32),
            pltpu.VMEM((subs, rows, width), F32),
            pltpu.VMEM((subs, rows + 2 * HALO, width), F32),
            pltpu.VMEM((bands, height, 128), F32),
        ],
        compiler_params=params(),
        name="grid_and_step",
    )(steps, received, image, dual)


def weight_matrices(conv_first, conv_middle, conv_last):
    ci = conv_first.shape[1]
    co = conv_last.shape[0]
    first = conv_first.transpose(3, 2, 1, 0)
    middle = conv_middle.transpose(3, 2, 1, 0)
    last = conv_last[:, :, ::-1].transpose(3, 1, 2, 0).reshape(3, CH, 3 * co)
    ins = GROUP + 2
    outs = GROUP * co

    def kernel(first_ref, mid_ref, last_ref, one_ref, two_ref, three_ref):
        zero = jnp.zeros((ci, CH), F32)
        rows = []
        for t in range(3):
            for r in range(ins):
                parts = []
                for phase in range(2):
                    for k in range(GROUP // 2):
                        dy = r - 2 * k - phase
                        parts.append(first_ref[t, dy].astype(F32) if 0 <= dy < 3 else zero)
                rows.append(jnp.concatenate(parts, axis=1))
        one_ref[...] = jnp.concatenate(rows, axis=0).astype(BF)
        zero = jnp.zeros((CH, CH), BF)
        for t in range(3):
            for r in range(GROUP // 2 + 2):
                parts = [
                    mid_ref[t, r - k] if 0 <= r - k < 3 else zero for k in range(GROUP // 2)
                ]
                at = (t * (GROUP // 2 + 2) + r) * CH
                two_ref[at : at + CH, :] = jnp.concatenate(parts, axis=1)
        three_ref[...] = jnp.zeros(three_ref.shape, BF)
        lane = lax.broadcasted_iota(jnp.int32, (CH, 128), 1)
        keep = jnp.where(lane < outs, 1.0, 0.0)
        for r in range(ins):
            taps = []
            for t in range(3):
                base = jnp.concatenate(
                    [last_ref[t].astype(F32), jnp.zeros((CH, 128 - 3 * co), F32)], axis=1
                )
                taps.append(pltpu.roll(base, (r - 2) * co % 128, 1) * keep)
            block = jnp.concatenate([taps[0] + pltpu.roll(taps[1], outs, 1), taps[2]], axis=1)
            if r < GROUP:
                at = (r % 2 * (GROUP // 2) + r // 2) * CH
            else:
                at = GROUP * CH + (r - GROUP) * 2 * CH
            three_ref[at : at + CH, :] = block.astype(BF)

    return pl.pallas_call(
        kernel,
        out_shape=[
            jax.ShapeDtypeStruct((3 * ins * ci, GROUP * CH), BF),
            jax.ShapeDtypeStruct((3 * (GROUP // 2 + 2) * CH, GROUP // 2 * CH), BF),
            jax.ShapeDtypeStruct(((GROUP + 4) * CH, 256), BF),
        ],
        in_specs=[vmem()] * 3,
        out_specs=[vmem()] * 3,
        compiler_params=params(),
        cost_estimate=pl.CostEstimate(flops=1 << 20, bytes_accessed=1 << 20, transcendentals=0),
        name="weight_matrices",
    )(first, middle, last)


def denoise(pieces, first, middle, last, subs, bands, band_rows, width):
    channels = subs * bands
    piece = band_rows + 2 * HALO
    groups = band_rows // GROUP + 1
    cols = width + 2 * PAD
    lanes = -(-cols // 128) * 128
    tall = -(-(cols + 2 * HALO) // 16) * 16
    in_rows = GROUP + 2
    facets = lax.axis_size("facet")

    def kernel(first_ref, mid_ref, last_ref, *rest):
        piece_refs = rest[:bands]
        out_refs = rest[bands : 2 * bands]
        x_ref, one_ref, two_ref, noise_ref = rest[2 * bands :]
        me = lax.axis_index("band")
        facet = lax.axis_index("facet")
        x_ref[:, piece * channels :, :] = jnp.zeros((lanes // 128, 2 * channels, 128), F32)
        one_ref[groups] = jnp.zeros(one_ref.shape[1:], BF)
        place_row = lax.broadcasted_iota(jnp.int32, (2 * subs * HALO, lanes), 0)
        place_lane = lax.broadcasted_iota(jnp.int32, (2 * subs * HALO, lanes), 1)
        side = place_row // HALO % 2
        spot = jnp.where(side == 0, PAD - HALO, PAD + width) + place_row % HALO
        for k in range(bands):
            band = lax.rem(me + bands - k, bands)
            for sub in range(subs):
                put = jnp.where(
                    (place_lane == spot) & (place_row // (2 * HALO) == sub), 1.0, 0.0
                ).astype(BF)
                halo = contract_first(piece_refs[k][subs * piece :, 0:128], put)[:piece]
                own = piece_refs[k][sub * piece : (sub + 1) * piece, :].astype(F32)
                own = jnp.concatenate([own, jnp.zeros((piece, lanes - width), F32)], axis=1)
                own = pltpu.roll(own, PAD, 1) + halo
                for part in range(lanes // 128):
                    x_ref[part, pl.ds(band * subs + sub, piece, stride=channels), :] = own[
                        :, part * 128 : (part + 1) * 128
                    ]

        col = lax.broadcasted_iota(jnp.int32, (1, lanes), 1) - PAD
        inside = ((col >= 0) | (facet > 0)) & ((col < width) | (facet < facets - 1))
        inside = jnp.where(inside, 1.0, 0.0)
        lane_id = lax.broadcasted_iota(jnp.int32, (1, GROUP * CH), 1)
        lane_row = lane_id // (GROUP // 2 * CH) + 2 * (lane_id // CH % (GROUP // 2))

        def layer_one(g):
            top = g * GROUP * channels
            x = jnp.concatenate(
                [x_ref[part, top : top + in_rows * channels, :] for part in range(lanes // 128)], axis=1
            )
            stack = jnp.concatenate(
                [pltpu.roll(x, 1, 1) * inside, x * inside, pltpu.roll(x, lanes - 1, 1) * inside], axis=0
            )
            stack = stack.astype(BF).T[:cols]
            hidden = dot(stack, first_ref[...])
            row = lane_row + (g * GROUP + 1 - HALO) + me * band_rows
            keep = jnp.where((row >= 0) & (row < band_rows * bands), 1.0, 0.0)
            one_ref[g, 0:cols, :] = (jnp.maximum(hidden, 0.0) * keep).astype(BF)

        block = GROUP // 2 * CH

        def layer_two(g):
            row = lane_row + (g * GROUP - 1) + me * band_rows
            keep = jnp.where((row >= 0) & (row < band_rows * bands), 1.0, 0.0)
            for phase in range(2):
                here = one_ref[g, :, phase * block : (phase + 1) * block]
                after = one_ref[g + 1, :, phase * block : phase * block + 2 * CH]
                parts = []
                for t in range(3):
                    parts += [here[2 * t : 2 * t + cols], after[2 * t : 2 * t + cols]]
                hidden = dot(jnp.concatenate(parts, axis=1), mid_ref[...])
                part = keep[:, phase * block : (phase + 1) * block]
                two_ref[g, :, phase * block : (phase + 1) * block] = (
                    jnp.maximum(hidden, 0.0) * part
                ).astype(BF)

        out_ch = channels * GROUP
        out_col = lax.broadcasted_iota(jnp.int32, (1, width), 1)
        has_left = jnp.where((out_col > 0) | (facet > 0), 1.0, 0.0)
        has_right = jnp.where((out_col < width - 1) | (facet < facets - 1), 1.0, 0.0)

        def layer_three(g):
            hidden = jnp.concatenate(
                [
                    two_ref[g],
                    two_ref[g + 1, :, 0 : 2 * CH],
                    two_ref[g + 1, :, block : block + 2 * CH],
                ],
                axis=1,
            )
            y = dot(hidden, last_ref[...]).T
            base = PAD - 2
            noise = (
                y[:out_ch, base - 1 : base - 1 + width] * has_left
                + y[out_ch : 2 * out_ch, base : base + width]
                + y[2 * out_ch : 3 * out_ch, base + 1 : base + 1 + width] * has_right
            )
            for part in range(width // 128):
                noise_ref[part, g * out_ch : (g + 1) * out_ch, :] = noise[
                    :, part * 128 : (part + 1) * 128
                ]

        for g in range(groups + 4):
            if g < groups:
                layer_one(g)
            if 0 <= g - 2 < groups:
                layer_two(g - 2)
            if 0 <= g - 4 < groups - 1:
                layer_three(g - 4)
        for k in range(bands):
            band = lax.rem(me + k, bands)
            for sub in range(subs):
                for part in range(width // 128):
                    out_refs[k][
                        sub * band_rows : (sub + 1) * band_rows, part * 128 : (part + 1) * 128
                    ] = noise_ref[
                        part, pl.ds(band * subs + sub, band_rows, stride=channels), :
                    ].astype(BF)

    return pl.pallas_call(
        kernel,
        out_shape=[jax.ShapeDtypeStruct((subs * band_rows, width), BF)] * bands,
        in_specs=[vmem()] * (3 + bands),
        out_specs=[vmem()] * bands,
        scratch_shapes=[
            pltpu.VMEM((lanes // 128, (groups * GROUP + 2) * channels, 128), F32),
            pltpu.VMEM((groups + 1, tall, GROUP * CH), BF),
            pltpu.VMEM((groups, cols, GROUP * CH), BF),
            pltpu.VMEM((width // 128, band_rows * channels, 128), F32),
        ],
        compiler_params=params(32),
        name="denoise",
    )(first, middle, last, *pieces)


def finish(shifted, noises, bands):
    subs, rows, width = shifted.shape
    band_rows = rows // bands

    def kernel(shift_ref, *rest):
        noise_refs = rest[:bands]
        img_ref, dual_ref = rest[bands:]
        me = lax.axis_index("band")
        for k in range(bands):
            start = pl.multiple_of(lax.rem(me + bands - k, bands) * band_rows, band_rows)
            for sub in range(subs):
                noise = noise_refs[k][sub * band_rows : (sub + 1) * band_rows, :].astype(F32)
                shifted_part = shift_ref[sub, pl.ds(start, band_rows), :]
                image_next = jnp.maximum(shifted_part - noise, 0.0)
                img_ref[sub, pl.ds(start, band_rows), :] = image_next
                dual_ref[sub, pl.ds(start, band_rows), :] = shifted_part - image_next

    return pl.pallas_call(
        kernel,
        out_shape=[jax.ShapeDtypeStruct(shifted.shape, F32)] * 2,
        in_specs=[vmem()] * (1 + bands),
        out_specs=[vmem()] * 2,
        compiler_params=params(),
        name="finish",
    )(shifted, *noises)


def exchange(parts, bands):
    return [parts[0]] + [
        lax.ppermute(parts[k], "band", [(i, (i + k) % bands) for i in range(bands)])
        for k in range(1, bands)
    ]


def body(
    visibility,
    uv_positions,
    destinations,
    column_slots,
    image_cube,
    dual_cube,
    step_sizes,
    conv_first,
    conv_middle,
    conv_last,
):
    facets = lax.axis_size("facet")
    bands = lax.axis_size("band")
    subs, blocks = visibility.shape[:2]
    rows, width = image_cube.shape[1:]
    pairs = max(2, 2 * blocks // facets) // 2
    packed = pack_blocks(
        visibility,
        uv_positions,
        destinations,
        column_slots,
        image_cube,
        dual_cube,
        step_sizes,
        facets,
        pairs,
    )
    received = lax.all_to_all(packed, "facet", split_axis=0, concat_axis=0, tiled=True)
    weights = weight_matrices(conv_first, conv_middle, conv_last)
    shifted, *pieces = grid_and_step(received, image_cube, dual_cube, step_sizes, pairs, bands)
    pieces = exchange(pieces, bands)
    noises = denoise(pieces, *weights, subs, bands, rows // bands, width)
    return tuple(finish(shifted, exchange(noises, bands), bands))


def solution(mesh):
    return jax.shard_map(
        body,
        mesh=mesh,
        in_specs=(
            P("band", "facet", None, None),
            P("band", "facet", None, None),
            P("band", "facet", None),
            P("band", "facet"),
            P("band", None, "facet"),
            P("band", None, "facet"),
            P("band"),
            P(),
            P(),
            P(),
        ),
        out_specs=(P("band", None, "facet"), P("band", None, "facet")),
        check_vma=False,
    )
```

```python
import jax
import jax.numpy as jnp
from jax import lax
from jax.experimental import pallas as pl
from jax.experimental.pallas import tpu as pltpu
from jax.sharding import PartitionSpec as P

P_SIZE = 256
KW = 8
S = 64
HALF = P_SIZE // 2
CENTRE = (P_SIZE - KW + HALF) // 2
HALO = 4
PAD = 8
GROUP = 8
CH = 64
CHUNKS = 4
DEPTH = 2
BF = jnp.bfloat16
F32 = jnp.float32


def params(mib=24):
    return pltpu.CompilerParams(vmem_limit_bytes=mib << 20)


def vmem():
    return pl.BlockSpec(memory_space=pltpu.VMEM)


def smem():
    return pl.BlockSpec(memory_space=pltpu.SMEM)


def taps(row, col):
    offset = col - row
    value = jnp.exp(-0.5 * ((offset.astype(F32) - (KW - 1) / 2.0) / (KW / 4.0)) ** 2)
    return jnp.where((offset >= 0) & (offset < KW), value, 0.0).astype(BF)


def contract_last(a, b):
    return lax.dot_general(a, b, (((1,), (1,)), ((), ())), preferred_element_type=F32)


def contract_first(a, b):
    return lax.dot_general(a, b, (((0,), (0,)), ((), ())), preferred_element_type=F32)


def dot(a, b):
    return jnp.dot(a, b, preferred_element_type=F32)


def tap_matrix(size):
    shape = (size, size)
    return taps(lax.broadcasted_iota(jnp.int32, shape, 1), lax.broadcasted_iota(jnp.int32, shape, 0))


def pack_blocks(
    visibility, uv_positions, destinations, column_slots, image, dual, steps, facets, pairs
):
    rows, width = image.shape[1:]
    subs, blocks = visibility.shape[:2]
    vis_rows = subs * pairs * S
    pos_rows = -(-2 * subs * pairs // 16) * 16

    chunk = blocks // CHUNKS
    halo_rows = 2 * HALO * subs * (rows // 128)

    def kernel(dest_hbm, slot_hbm, vis_hbm, pos_hbm, img_hbm, dual_hbm, step_hbm, *rest):
        out_refs, rest = rest[:facets], rest[facets:]
        dest_ref, slot_ref, vis_ref, pos_ref, edge_ref, step_ref, count_ref = rest[:7]
        place_ref, side_ref, main_ref, halo_ref, sems = rest[7:]
        small = [
            pltpu.make_async_copy(dest_hbm, dest_ref, sems.at[CHUNKS]),
            pltpu.make_async_copy(slot_hbm, slot_ref, sems.at[CHUNKS + 1]),
            pltpu.make_async_copy(pos_hbm, pos_ref, sems.at[CHUNKS + 2]),
        ]
        large = [
            pltpu.make_async_copy(
                vis_hbm.at[:, pl.ds(c * chunk, chunk)], vis_ref.at[:, pl.ds(c * chunk, chunk)], sems.at[c]
            )
            for c in range(CHUNKS)
        ]
        edges = [
            pltpu.make_async_copy(step_hbm, step_ref, sems.at[CHUNKS + 3]),
        ] + [
            pltpu.make_async_copy(
                ref.at[:, :, pl.ds(at, 128)], edge_ref.at[n, side], sems.at[CHUNKS + 4 + 2 * n + side]
            )
            for n, ref in enumerate((img_hbm, dual_hbm))
            for side, at in enumerate((0, width - 128))
        ]
        for copy in small + large + edges:
            copy.start()
        side_ref[...] = jnp.zeros(side_ref.shape, BF)
        place_ref[...] = jnp.zeros(place_ref.shape, F32)
        for n in range(subs * facets):
            count_ref[n] = 0
        wide = facets * 4 * HALO
        cell_row = lax.broadcasted_iota(jnp.int32, (4 * HALO, 2 * S), 0)
        cell_lane = lax.broadcasted_iota(jnp.int32, (4 * HALO, 2 * S), 1)
        cell = cell_row % HALO + (width - KW - HALO + 1) * (cell_row // HALO % 2) - CENTRE
        cell = jnp.where(cell_lane // S == cell_row // (2 * HALO), cell, 2 * P_SIZE)
        cell = cell.astype(F32).astype(BF)
        lane = lax.broadcasted_iota(jnp.int32, (1, wide), 1)
        mine = [
            jnp.where(lane // (2 * HALO) % 2 == block, 1.0, 0.0).astype(BF) for block in range(2)
        ]
        row_id = lax.broadcasted_iota(jnp.int32, (rows, 2 * S), 0).astype(F32).astype(BF)
        yes = jnp.ones((), BF)
        no = jnp.zeros((), BF)
        shape = (wide, facets * 2 * HALO)
        src = lax.broadcasted_iota(jnp.int32, shape, 0)
        dst = lax.broadcasted_iota(jnp.int32, shape, 1)
        halo_side = dst // HALO % 2
        meets = (src // (4 * HALO) == dst // (2 * HALO) + 2 * halo_side - 1) & (
            src // HALO % 2 == 1 - halo_side
        )
        offset = dst % HALO - src % HALO + (KW - 1) * (1 - halo_side)
        v_taps = jnp.where(meets, taps(0, offset).astype(F32), 0.0).astype(BF)
        u_taps = tap_matrix(rows)
        me = lax.axis_index("facet")
        shape = (128, facets * 2 * HALO)
        src = lax.broadcasted_iota(jnp.int32, shape, 0)
        dst = lax.broadcasted_iota(jnp.int32, shape, 1)
        halo_side = dst // HALO % 2
        pick = [
            jnp.where(
                (src == dst % HALO + (128 - HALO) * side)
                & (halo_side == 1 - side)
                & (dst // (2 * HALO) == me + 2 * side - 1),
                1.0,
                0.0,
            ).astype(BF)
            for side in range(2)
        ]
        for copy in small:
            copy.wait()

        def one(n, carry):
            for sub in range(subs):
                facet = dest_ref[sub, n]
                slot = slot_ref[sub, n]
                count = count_ref[sub * facets + facet]
                count_ref[sub * facets + facet] = count + 1
                pair = count // 2
                side = count - 2 * pair
                side_ref[side, facet, sub * pairs + pair] = vis_ref[sub, n]
                where = facet * pos_rows + sub * pairs + pair
                place = pos_ref[sub, n].astype(F32)
                shift = (slot * HALF - CENTRE).astype(F32)
                place_ref[side, pl.ds(where, 1), :] = place[0:1]
                place_ref[side, pl.ds(where + subs * pairs, 1), :] = place[1:2] + shift
            return carry

        for c in range(CHUNKS):
            large[c].wait()
            lax.fori_loop(c * chunk, (c + 1) * chunk, one, 0, unroll=4)
        for facet in range(facets):
            both = jnp.concatenate([side_ref[0, facet], side_ref[1, facet]], axis=2)
            main_ref[facet, :vis_rows, :] = both.reshape(vis_rows, 2 * S)
        both = jnp.concatenate([place_ref[0], place_ref[1]], axis=1)
        main_ref[:, vis_rows:, :] = both.astype(BF).reshape(facets, pos_rows, 2 * S)
        spot = lax.axis_index("facet")
        main_rows = vis_rows + pos_rows
        sent = [
            pltpu.make_async_copy(
                main_ref.at[spot ^ k], out_refs[k].at[pl.ds(0, main_rows)], sems.at[CHUNKS + 8 + k]
            )
            for k in range(facets)
        ]
        sent_halo = [
            pltpu.make_async_copy(
                halo_ref.at[spot ^ k],
                out_refs[k].at[pl.ds(main_rows, halo_rows)],
                sems.at[CHUNKS + 8 + facets + k],
            )
            for k in range(facets)
        ]
        for copy in sent:
            copy.start()

        for copy in edges:
            copy.wait()
        halos = []
        for sub in range(subs):
            hots, parts = [], []
            for facet in range(facets):
                for pair in range(pairs):
                    at = sub * pairs + pair
                    where = facet * pos_rows + at
                    u_row = both[where : where + 1].astype(BF)
                    v_row = both[where + subs * pairs : where + subs * pairs + 1].astype(BF)
                    hots.append(jnp.where(row_id == u_row, yes, no))
                    hot = jnp.where(cell == v_row, yes, no)
                    found = contract_last(main_ref[facet, at * S : (at + 1) * S, :], hot)
                    left, right = facet * 4 * HALO, (facets - facet - 1) * 4 * HALO
                    row = [jnp.zeros((S, left), F32)] if left else []
                    row += [found]
                    row += [jnp.zeros((S, right), F32)] if right else []
                    found = jnp.concatenate(row, axis=1).astype(BF)
                    parts += [found * mine[0], found * mine[1]]
            total = dot(jnp.concatenate(hots, axis=1), jnp.concatenate(parts, axis=0))
            gradient = dot(dot(u_taps, total.astype(BF)).astype(BF), v_taps)
            halo = -step_ref[sub] * gradient
            for side in range(2):
                base = edge_ref[0, side, sub] + edge_ref[1, side, sub]
                halo += dot(base.astype(BF), pick[side])
            halos.append(halo.T.reshape(facets, 2 * HALO, rows))
        halo = jnp.concatenate(halos, axis=1).astype(BF)
        height = 2 * HALO * subs
        for part in range(rows // 128):
            halo_ref[:, part * height : (part + 1) * height, :] = halo[
                :, :, part * 128 : (part + 1) * 128
            ]
        for copy in sent_halo:
            copy.start()
        for copy in sent + sent_halo:
            copy.wait()

    hbm = pl.BlockSpec(memory_space=pltpu.HBM)
    return pl.pallas_call(
        kernel,
        out_shape=[jax.ShapeDtypeStruct((vis_rows + pos_rows + halo_rows, 2 * S), BF)] * facets,
        in_specs=[hbm] * 7,
        out_specs=[hbm] * facets,
        scratch_shapes=[
            pltpu.SMEM((subs, blocks), jnp.int32),
            pltpu.SMEM((subs, blocks), jnp.int32),
            pltpu.VMEM((subs, blocks, S, S), BF),
            pltpu.VMEM((subs, blocks, 2, S), jnp.int32),
            pltpu.VMEM((2, 2, subs, rows, 128), F32),
            pltpu.SMEM((subs,), F32),
            pltpu.SMEM((subs * facets,), jnp.int32),
            pltpu.VMEM((2, facets * pos_rows, S), F32),
            pltpu.VMEM((2, facets, subs * pairs, S, S), BF),
            pltpu.VMEM((facets, vis_rows + pos_rows, 2 * S), BF),
            pltpu.VMEM((facets, halo_rows, 2 * S), BF),
            pltpu.SemaphoreType.DMA((CHUNKS + 8 + 2 * facets,)),
        ],
        compiler_params=params(60),
        name="pack_blocks",
    )(destinations[..., 0], column_slots, visibility, uv_positions, image, dual, steps)


def grid_and_step(received, image, dual, steps, pairs, bands):
    facets = len(received)
    subs, rows, width = image.shape
    vis_rows = subs * pairs * S
    per = 4
    sources = per // pairs
    band_rows = rows // bands
    piece = band_rows + 2 * HALO
    pos_rows = -(-2 * subs * pairs // 16) * 16
    height = 2 * HALO * subs

    def kernel(step_ref, img_ref, dual_ref, *rest):
        rec_refs, rest = rest[:facets], rest[facets:]
        shift_ref, rest = rest[0], rest[1:]
        piece_refs = rest[:bands]
        place_ref, acc_ref, den_ref, halo_ref = rest[bands:]
        for source in range(facets):
            place_ref[source] = rec_refs[source][vis_rows : vis_rows + pos_rows, :].astype(F32)
        one = jnp.ones((), BF)
        none = jnp.zeros((), BF)
        lane = lax.broadcasted_iota(jnp.int32, (1, 2 * S), 1)
        left = jnp.where(lane < S, 1.0, 0.0).astype(BF)
        right = jnp.where(lane < S, 0.0, 1.0).astype(BF)
        zero = jnp.zeros((2 * S, 2 * S), BF)
        row_id = lax.broadcasted_iota(jnp.int32, (rows, 2 * S), 0).astype(F32).astype(BF)
        col_id = (lax.broadcasted_iota(jnp.int32, (width, 2 * S), 0) - CENTRE).astype(F32).astype(BF)

        spreads = [[] for _ in range(subs)]
        hots = [[] for _ in range(subs)]
        for it in range(facets // sources):
            for sub in range(subs):
                first, second = [], []
                for q in range(per):
                    source = it * sources + q // pairs
                    at = sub * pairs + q % pairs
                    block = rec_refs[source][at * S : (at + 1) * S, :]
                    diag = jnp.concatenate([block * left, block * right], axis=0)
                    u_row = place_ref[source, at : at + 1, :].astype(BF)
                    v_row = place_ref[source, at + subs * pairs : at + subs * pairs + 1, :].astype(BF)
                    u_hot = jnp.where(row_id == u_row, one, none)
                    v_hot = jnp.where(col_id == v_row, one, none)
                    first.append((u_hot, diag))
                    second.append(v_hot)
                spread = []
                for q in range(0, per, 2):
                    hot = jnp.concatenate([first[q][0], first[q + 1][0]], axis=1)
                    block = jnp.concatenate(
                        [
                            jnp.concatenate([first[q][1], zero], axis=1),
                            jnp.concatenate([zero, first[q + 1][1]], axis=1),
                        ],
                        axis=0,
                    )
                    spread.append(dot(hot, block).astype(BF))
                spreads[sub] += spread
                hots[sub] += second
                if it % DEPTH == DEPTH - 1:
                    term = contract_last(
                        jnp.concatenate(spreads[sub], axis=1), jnp.concatenate(hots[sub], axis=1)
                    )
                    acc_ref[sub] = term if it < DEPTH else acc_ref[sub] + term
                    spreads[sub], hots[sub] = [], []

        u_taps = tap_matrix(rows)
        v_taps = taps(
            lax.broadcasted_iota(jnp.int32, (width, width), 0),
            lax.broadcasted_iota(jnp.int32, (width, width), 1),
        )
        den_ref[...] = jnp.zeros(den_ref.shape, F32)
        me = lax.axis_index("band")
        for sub in range(subs):
            total = acc_ref[sub]
            high = total.astype(BF)
            low = (total - high.astype(F32)).astype(BF)
            half = dot(u_taps, high) + dot(u_taps, low)
            gradient = dot(half.astype(BF), v_taps)
            stepped = img_ref[sub] - step_ref[sub] * gradient
            shifted = stepped + dual_ref[sub]
            shift_ref[sub] = shifted
            den_ref[sub, HALO : HALO + rows, :] = shifted
        halo = sum(ref[vis_rows + pos_rows :, :].astype(F32) for ref in rec_refs)
        parts = [halo[n * height : (n + 1) * height] for n in range(rows // 128)]
        halo = jnp.concatenate(parts + [jnp.zeros((height, 128), F32)], axis=1)
        steps_in = 128 // band_rows
        for n in range(steps_in):
            shift = (HALO - n * band_rows) % (rows + 128)
            moved = pltpu.roll(halo, shift, 1)
            for tile in range(bands // steps_in):
                halo_ref[tile * steps_in + n] = moved[:, tile * 128 : (tile + 1) * 128]
        blank = jnp.zeros((height, width - 128), F32)
        for k in range(bands):
            band = lax.rem(me + k, bands)
            start = pl.multiple_of(band * band_rows, band_rows)
            piece_refs[k][...] = jnp.concatenate(
                [den_ref[sub, pl.ds(start, piece), :] for sub in range(subs)]
                + [jnp.concatenate([halo_ref[band], blank], axis=1)],
                axis=0,
            ).astype(BF)

    return pl.pallas_call(
        kernel,
        out_shape=[jax.ShapeDtypeStruct(image.shape, F32)]
        + [jax.ShapeDtypeStruct((subs * piece + height, width), BF)] * bands,
        in_specs=[smem()] + [vmem()] * (2 + facets),
        out_specs=[vmem()] * (1 + bands),
        scratch_shapes=[
            pltpu.VMEM((facets, pos_rows, 2 * S), F32),
            pltpu.VMEM((subs, rows, width), F32),
            pltpu.VMEM((subs, rows + 2 * HALO, width), F32),
            pltpu.VMEM((bands, height, 128), F32),
        ],
        compiler_params=params(),
        name="grid_and_step",
    )(steps, image, dual, *received)


def weight_matrices(conv_first, conv_middle, conv_last):
    ci = conv_first.shape[1]
    co = conv_last.shape[0]
    first = conv_first.transpose(3, 2, 1, 0)
    middle = conv_middle.transpose(3, 2, 1, 0)
    last = conv_last[:, :, ::-1].transpose(3, 1, 2, 0).reshape(3, CH, 3 * co)
    ins = GROUP + 2
    outs = GROUP * co

    def kernel(first_ref, mid_ref, last_ref, one_ref, two_ref, three_ref):
        zero = jnp.zeros((ci, CH), F32)
        rows = []
        for t in range(3):
            for r in range(ins):
                parts = []
                for phase in range(2):
                    for k in range(GROUP // 2):
                        dy = r - 2 * k - phase
                        parts.append(first_ref[t, dy].astype(F32) if 0 <= dy < 3 else zero)
                rows.append(jnp.concatenate(parts, axis=1))
        one_ref[...] = jnp.concatenate(rows, axis=0).astype(BF)
        zero = jnp.zeros((CH, CH), BF)
        for t in range(3):
            for r in range(GROUP // 2 + 2):
                parts = [
                    mid_ref[t, r - k] if 0 <= r - k < 3 else zero for k in range(GROUP // 2)
                ]
                at = (t * (GROUP // 2 + 2) + r) * CH
                two_ref[at : at + CH, :] = jnp.concatenate(parts, axis=1)
        three_ref[...] = jnp.zeros(three_ref.shape, BF)
        lane = lax.broadcasted_iota(jnp.int32, (CH, 128), 1)
        keep = jnp.where(lane < outs, 1.0, 0.0)
        for r in range(ins):
            taps = []
            for t in range(3):
                base = jnp.concatenate(
                    [last_ref[t].astype(F32), jnp.zeros((CH, 128 - 3 * co), F32)], axis=1
                )
                taps.append(pltpu.roll(base, (r - 2) * co % 128, 1) * keep)
            block = jnp.concatenate([taps[0] + pltpu.roll(taps[1], outs, 1), taps[2]], axis=1)
            if r < GROUP:
                at = (r % 2 * (GROUP // 2) + r // 2) * CH
            else:
                at = GROUP * CH + (r - GROUP) * 2 * CH
            three_ref[at : at + CH, :] = block.astype(BF)

    return pl.pallas_call(
        kernel,
        out_shape=[
            jax.ShapeDtypeStruct((3 * ins * ci, GROUP * CH), BF),
            jax.ShapeDtypeStruct((3 * (GROUP // 2 + 2) * CH, GROUP // 2 * CH), BF),
            jax.ShapeDtypeStruct(((GROUP + 4) * CH, 256), BF),
        ],
        in_specs=[vmem()] * 3,
        out_specs=[vmem()] * 3,
        compiler_params=params(),
        cost_estimate=pl.CostEstimate(flops=1 << 20, bytes_accessed=1 << 20, transcendentals=0),
        name="weight_matrices",
    )(first, middle, last)


def denoise(pieces, first, middle, last, subs, bands, band_rows, width):
    channels = subs * bands
    piece = band_rows + 2 * HALO
    groups = band_rows // GROUP + 1
    cols = width + 2 * PAD
    lanes = -(-cols // 128) * 128
    tall = -(-(cols + 2 * HALO) // 16) * 16
    in_rows = GROUP + 2
    facets = lax.axis_size("facet")

    def kernel(first_ref, mid_ref, last_ref, *rest):
        piece_refs = rest[:bands]
        out_refs = rest[bands : 2 * bands]
        x_ref, one_ref, two_ref, noise_ref = rest[2 * bands :]
        me = lax.axis_index("band")
        facet = lax.axis_index("facet")
        x_ref[:, piece * channels :, :] = jnp.zeros((lanes // 128, 2 * channels, 128), F32)
        one_ref[groups] = jnp.zeros(one_ref.shape[1:], BF)
        place_row = lax.broadcasted_iota(jnp.int32, (2 * subs * HALO, lanes), 0)
        place_lane = lax.broadcasted_iota(jnp.int32, (2 * subs * HALO, lanes), 1)
        side = place_row // HALO % 2
        spot = jnp.where(side == 0, PAD - HALO, PAD + width) + place_row % HALO
        for k in range(bands):
            band = lax.rem(me + bands - k, bands)
            for sub in range(subs):
                put = jnp.where(
                    (place_lane == spot) & (place_row // (2 * HALO) == sub), 1.0, 0.0
                ).astype(BF)
                halo = contract_first(piece_refs[k][subs * piece :, 0:128], put)[:piece]
                own = piece_refs[k][sub * piece : (sub + 1) * piece, :].astype(F32)
                own = jnp.concatenate([own, jnp.zeros((piece, lanes - width), F32)], axis=1)
                own = pltpu.roll(own, PAD, 1) + halo
                for part in range(lanes // 128):
                    x_ref[part, pl.ds(band * subs + sub, piece, stride=channels), :] = own[
                        :, part * 128 : (part + 1) * 128
                    ]

        col = lax.broadcasted_iota(jnp.int32, (1, lanes), 1) - PAD
        inside = ((col >= 0) | (facet > 0)) & ((col < width) | (facet < facets - 1))
        inside = jnp.where(inside, 1.0, 0.0)
        lane_id = lax.broadcasted_iota(jnp.int32, (1, GROUP * CH), 1)
        lane_row = lane_id // (GROUP // 2 * CH) + 2 * (lane_id // CH % (GROUP // 2))

        def layer_one(g):
            top = g * GROUP * channels
            x = jnp.concatenate(
                [x_ref[part, top : top + in_rows * channels, :] for part in range(lanes // 128)], axis=1
            )
            stack = jnp.concatenate(
                [pltpu.roll(x, 1, 1) * inside, x * inside, pltpu.roll(x, lanes - 1, 1) * inside], axis=0
            )
            stack = stack.astype(BF).T[:cols]
            hidden = dot(stack, first_ref[...])
            row = lane_row + (g * GROUP + 1 - HALO) + me * band_rows
            keep = jnp.where((row >= 0) & (row < band_rows * bands), 1.0, 0.0)
            one_ref[g, 0:cols, :] = (jnp.maximum(hidden, 0.0) * keep).astype(BF)

        block = GROUP // 2 * CH

        def layer_two(g):
            row = lane_row + (g * GROUP - 1) + me * band_rows
            keep = jnp.where((row >= 0) & (row < band_rows * bands), 1.0, 0.0)
            for phase in range(2):
                here = one_ref[g, :, phase * block : (phase + 1) * block]
                after = one_ref[g + 1, :, phase * block : phase * block + 2 * CH]
                parts = []
                for t in range(3):
                    parts += [here[2 * t : 2 * t + cols], after[2 * t : 2 * t + cols]]
                hidden = dot(jnp.concatenate(parts, axis=1), mid_ref[...])
                part = keep[:, phase * block : (phase + 1) * block]
                two_ref[g, :, phase * block : (phase + 1) * block] = (
                    jnp.maximum(hidden, 0.0) * part
                ).astype(BF)

        out_ch = channels * GROUP
        out_col = lax.broadcasted_iota(jnp.int32, (1, width), 1)
        has_left = jnp.where((out_col > 0) | (facet > 0), 1.0, 0.0)
        has_right = jnp.where((out_col < width - 1) | (facet < facets - 1), 1.0, 0.0)

        def layer_three(g):
            hidden = jnp.concatenate(
                [
                    two_ref[g],
                    two_ref[g + 1, :, 0 : 2 * CH],
                    two_ref[g + 1, :, block : block + 2 * CH],
                ],
                axis=1,
            )
            y = dot(hidden, last_ref[...]).T
            base = PAD - 2
            noise = (
                y[:out_ch, base - 1 : base - 1 + width] * has_left
                + y[out_ch : 2 * out_ch, base : base + width]
                + y[2 * out_ch : 3 * out_ch, base + 1 : base + 1 + width] * has_right
            )
            for part in range(width // 128):
                noise_ref[part, g * out_ch : (g + 1) * out_ch, :] = noise[
                    :, part * 128 : (part + 1) * 128
                ]

        for g in range(groups + 4):
            if g < groups:
                layer_one(g)
            if 0 <= g - 2 < groups:
                layer_two(g - 2)
            if 0 <= g - 4 < groups - 1:
                layer_three(g - 4)
        for k in range(bands):
            band = lax.rem(me + k, bands)
            for sub in range(subs):
                for part in range(width // 128):
                    out_refs[k][
                        sub * band_rows : (sub + 1) * band_rows, part * 128 : (part + 1) * 128
                    ] = noise_ref[
                        part, pl.ds(band * subs + sub, band_rows, stride=channels), :
                    ].astype(BF)

    return pl.pallas_call(
        kernel,
        out_shape=[jax.ShapeDtypeStruct((subs * band_rows, width), BF)] * bands,
        in_specs=[vmem()] * (3 + bands),
        out_specs=[vmem()] * bands,
        scratch_shapes=[
            pltpu.VMEM((lanes // 128, (groups * GROUP + 2) * channels, 128), F32),
            pltpu.VMEM((groups + 1, tall, GROUP * CH), BF),
            pltpu.VMEM((groups, cols, GROUP * CH), BF),
            pltpu.VMEM((width // 128, band_rows * channels, 128), F32),
        ],
        compiler_params=params(32),
        name="denoise",
    )(first, middle, last, *pieces)


def finish(shifted, noises, bands):
    subs, rows, width = shifted.shape
    band_rows = rows // bands

    def kernel(shift_ref, *rest):
        noise_refs = rest[:bands]
        img_ref, dual_ref = rest[bands:]
        me = lax.axis_index("band")
        for k in range(bands):
            start = pl.multiple_of(lax.rem(me + bands - k, bands) * band_rows, band_rows)
            for sub in range(subs):
                noise = noise_refs[k][sub * band_rows : (sub + 1) * band_rows, :].astype(F32)
                shifted_part = shift_ref[sub, pl.ds(start, band_rows), :]
                image_next = jnp.maximum(shifted_part - noise, 0.0)
                img_ref[sub, pl.ds(start, band_rows), :] = image_next
                dual_ref[sub, pl.ds(start, band_rows), :] = shifted_part - image_next

    return pl.pallas_call(
        kernel,
        out_shape=[jax.ShapeDtypeStruct(shifted.shape, F32)] * 2,
        in_specs=[vmem()] * (1 + bands),
        out_specs=[vmem()] * 2,
        compiler_params=params(),
        name="finish",
    )(shifted, *noises)


def exchange(parts, bands):
    return [parts[0]] + [
        lax.ppermute(parts[k], "band", [(i, (i + k) % bands) for i in range(bands)])
        for k in range(1, bands)
    ]


def body(
    visibility,
    uv_positions,
    destinations,
    column_slots,
    image_cube,
    dual_cube,
    step_sizes,
    conv_first,
    conv_middle,
    conv_last,
):
    facets = lax.axis_size("facet")
    bands = lax.axis_size("band")
    subs, blocks = visibility.shape[:2]
    rows, width = image_cube.shape[1:]
    pairs = max(2, 2 * blocks // facets) // 2
    packed = pack_blocks(
        visibility,
        uv_positions,
        destinations,
        column_slots,
        image_cube,
        dual_cube,
        step_sizes,
        facets,
        pairs,
    )
    received = [packed[0]] + [
        lax.ppermute(packed[k], "facet", [(i, i ^ k) for i in range(facets)])
        for k in range(1, facets)
    ]
    weights = weight_matrices(conv_first, conv_middle, conv_last)
    shifted, *pieces = grid_and_step(received, image_cube, dual_cube, step_sizes, pairs, bands)
    pieces = exchange(pieces, bands)
    noises = denoise(pieces, *weights, subs, bands, rows // bands, width)
    return tuple(finish(shifted, exchange(noises, bands), bands))


def solution(mesh):
    return jax.shard_map(
        body,
        mesh=mesh,
        in_specs=(
            P("band", "facet", None, None),
            P("band", "facet", None, None),
            P("band", "facet", None),
            P("band", "facet"),
            P("band", None, "facet"),
            P("band", None, "facet"),
            P("band"),
            P(),
            P(),
            P(),
        ),
        out_specs=(P("band", None, "facet"), P("band", None, "facet")),
        check_vma=False,
    )
```

```python
import jax
import jax.numpy as jnp
from jax import lax
from jax.experimental import pallas as pl
from jax.experimental.pallas import tpu as pltpu
from jax.sharding import PartitionSpec as P

P_SIZE = 256
KW = 8
S = 64
HALF = P_SIZE // 2
CENTRE = (P_SIZE - KW + HALF) // 2
HALO = 4
PAD = 8
GROUP = 8
CH = 64
CHUNKS = 4
DEPTH = 2
BF = jnp.bfloat16
F32 = jnp.float32


def params(mib=24):
    return pltpu.CompilerParams(vmem_limit_bytes=mib << 20)


def vmem():
    return pl.BlockSpec(memory_space=pltpu.VMEM)


def smem():
    return pl.BlockSpec(memory_space=pltpu.SMEM)


def taps(row, col):
    offset = col - row
    value = jnp.exp(-0.5 * ((offset.astype(F32) - (KW - 1) / 2.0) / (KW / 4.0)) ** 2)
    return jnp.where((offset >= 0) & (offset < KW), value, 0.0).astype(BF)


def contract_last(a, b):
    return lax.dot_general(a, b, (((1,), (1,)), ((), ())), preferred_element_type=F32)


def contract_first(a, b):
    return lax.dot_general(a, b, (((0,), (0,)), ((), ())), preferred_element_type=F32)


def dot(a, b):
    return jnp.dot(a, b, preferred_element_type=F32)


def tap_matrix(size):
    shape = (size, size)
    return taps(lax.broadcasted_iota(jnp.int32, shape, 1), lax.broadcasted_iota(jnp.int32, shape, 0))


def pack_blocks(
    visibility, uv_positions, destinations, column_slots, image, dual, steps, facets, pairs
):
    rows, width = image.shape[1:]
    subs, blocks = visibility.shape[:2]
    vis_rows = subs * pairs * S
    pos_rows = -(-2 * subs * pairs // 16) * 16

    chunk = blocks // CHUNKS
    halo_rows = 2 * HALO * subs * (rows // 128)

    def kernel(dest_hbm, slot_hbm, vis_hbm, pos_hbm, img_hbm, dual_hbm, step_hbm, *rest):
        out_refs, rest = rest[:facets], rest[facets:]
        dest_ref, slot_ref, vis_ref, pos_ref, edge_ref, step_ref, count_ref = rest[:7]
        place_ref, side_ref, main_ref, halo_ref, sems = rest[7:]
        small = [
            pltpu.make_async_copy(dest_hbm, dest_ref, sems.at[CHUNKS]),
            pltpu.make_async_copy(slot_hbm, slot_ref, sems.at[CHUNKS + 1]),
            pltpu.make_async_copy(pos_hbm, pos_ref, sems.at[CHUNKS + 2]),
        ]
        large = [
            pltpu.make_async_copy(
                vis_hbm.at[:, pl.ds(c * chunk, chunk)], vis_ref.at[:, pl.ds(c * chunk, chunk)], sems.at[c]
            )
            for c in range(CHUNKS)
        ]
        edges = [
            pltpu.make_async_copy(step_hbm, step_ref, sems.at[CHUNKS + 3]),
        ] + [
            pltpu.make_async_copy(
                ref.at[:, :, pl.ds(at, 128)], edge_ref.at[n, side], sems.at[CHUNKS + 4 + 2 * n + side]
            )
            for n, ref in enumerate((img_hbm, dual_hbm))
            for side, at in enumerate((0, width - 128))
        ]
        for copy in small + large + edges:
            copy.start()
        side_ref[...] = jnp.zeros(side_ref.shape, BF)
        place_ref[...] = jnp.zeros(place_ref.shape, F32)
        for n in range(subs * facets):
            count_ref[n] = 0
        wide = facets * 4 * HALO
        cell_row = lax.broadcasted_iota(jnp.int32, (4 * HALO, 2 * S), 0)
        cell_lane = lax.broadcasted_iota(jnp.int32, (4 * HALO, 2 * S), 1)
        cell = cell_row % HALO + (width - KW - HALO + 1) * (cell_row // HALO % 2) - CENTRE
        cell = jnp.where(cell_lane // S == cell_row // (2 * HALO), cell, 2 * P_SIZE)
        cell = cell.astype(F32).astype(BF)
        lane = lax.broadcasted_iota(jnp.int32, (1, wide), 1)
        mine = [
            jnp.where(lane // (2 * HALO) % 2 == block, 1.0, 0.0).astype(BF) for block in range(2)
        ]
        row_id = lax.broadcasted_iota(jnp.int32, (rows, 2 * S), 0).astype(F32).astype(BF)
        yes = jnp.ones((), BF)
        no = jnp.zeros((), BF)
        shape = (wide, facets * 2 * HALO)
        src = lax.broadcasted_iota(jnp.int32, shape, 0)
        dst = lax.broadcasted_iota(jnp.int32, shape, 1)
        halo_side = dst // HALO % 2
        meets = (src // (4 * HALO) == dst // (2 * HALO) + 2 * halo_side - 1) & (
            src // HALO % 2 == 1 - halo_side
        )
        offset = dst % HALO - src % HALO + (KW - 1) * (1 - halo_side)
        v_taps = jnp.where(meets, taps(0, offset).astype(F32), 0.0).astype(BF)
        u_taps = tap_matrix(rows)
        me = lax.axis_index("facet")
        shape = (128, facets * 2 * HALO)
        src = lax.broadcasted_iota(jnp.int32, shape, 0)
        dst = lax.broadcasted_iota(jnp.int32, shape, 1)
        halo_side = dst // HALO % 2
        pick = [
            jnp.where(
                (src == dst % HALO + (128 - HALO) * side)
                & (halo_side == 1 - side)
                & (dst // (2 * HALO) == me + 2 * side - 1),
                1.0,
                0.0,
            ).astype(BF)
            for side in range(2)
        ]
        for copy in small:
            copy.wait()

        def one(n, carry):
            for sub in range(subs):
                facet = dest_ref[sub, n]
                slot = slot_ref[sub, n]
                count = count_ref[sub * facets + facet]
                count_ref[sub * facets + facet] = count + 1
                pair = count // 2
                side = count - 2 * pair
                side_ref[side, facet, sub * pairs + pair] = vis_ref[sub, n]
                where = facet * pos_rows + sub * pairs + pair
                place = pos_ref[sub, n].astype(F32)
                shift = (slot * HALF - CENTRE).astype(F32)
                place_ref[side, pl.ds(where, 1), :] = place[0:1]
                place_ref[side, pl.ds(where + subs * pairs, 1), :] = place[1:2] + shift
            return carry

        for c in range(CHUNKS):
            large[c].wait()
            lax.fori_loop(c * chunk, (c + 1) * chunk, one, 0, unroll=4)
        for facet in range(facets):
            both = jnp.concatenate([side_ref[0, facet], side_ref[1, facet]], axis=2)
            main_ref[facet, :vis_rows, :] = both.reshape(vis_rows, 2 * S)
        both = jnp.concatenate([place_ref[0], place_ref[1]], axis=1)
        main_ref[:, vis_rows:, :] = both.astype(BF).reshape(facets, pos_rows, 2 * S)
        spot = lax.axis_index("facet")
        main_rows = vis_rows + pos_rows
        sent = [
            pltpu.make_async_copy(
                main_ref.at[spot ^ k], out_refs[k].at[pl.ds(0, main_rows)], sems.at[CHUNKS + 8 + k]
            )
            for k in range(facets)
        ]
        sent_halo = [
            pltpu.make_async_copy(
                halo_ref.at[spot ^ k],
                out_refs[k].at[pl.ds(main_rows, halo_rows)],
                sems.at[CHUNKS + 8 + facets + k],
            )
            for k in range(facets)
        ]
        for copy in sent:
            copy.start()

        for copy in edges:
            copy.wait()
        halos = []
        for sub in range(subs):
            hots, parts = [], []
            for facet in range(facets):
                for pair in range(pairs):
                    at = sub * pairs + pair
                    where = facet * pos_rows + at
                    u_row = both[where : where + 1].astype(BF)
                    v_row = both[where + subs * pairs : where + subs * pairs + 1].astype(BF)
                    hots.append(jnp.where(row_id == u_row, yes, no))
                    hot = jnp.where(cell == v_row, yes, no)
                    found = contract_last(main_ref[facet, at * S : (at + 1) * S, :], hot)
                    left, right = facet * 4 * HALO, (facets - facet - 1) * 4 * HALO
                    row = [jnp.zeros((S, left), F32)] if left else []
                    row += [found]
                    row += [jnp.zeros((S, right), F32)] if right else []
                    found = jnp.concatenate(row, axis=1).astype(BF)
                    parts += [found * mine[0], found * mine[1]]
            total = dot(jnp.concatenate(hots, axis=1), jnp.concatenate(parts, axis=0))
            gradient = dot(dot(u_taps, total.astype(BF)).astype(BF), v_taps)
            halo = -step_ref[sub] * gradient
            for side in range(2):
                base = edge_ref[0, side, sub] + edge_ref[1, side, sub]
                halo += dot(base.astype(BF), pick[side])
            halos.append(halo.T.reshape(facets, 2 * HALO, rows))
        halo = jnp.concatenate(halos, axis=1).astype(BF)
        height = 2 * HALO * subs
        for part in range(rows // 128):
            halo_ref[:, part * height : (part + 1) * height, :] = halo[
                :, :, part * 128 : (part + 1) * 128
            ]
        for copy in sent_halo:
            copy.start()
        for copy in sent + sent_halo:
            copy.wait()

    hbm = pl.BlockSpec(memory_space=pltpu.HBM)
    return pl.pallas_call(
        kernel,
        out_shape=[jax.ShapeDtypeStruct((vis_rows + pos_rows + halo_rows, 2 * S), BF)] * facets,
        in_specs=[hbm] * 7,
        out_specs=[hbm] * facets,
        scratch_shapes=[
            pltpu.SMEM((subs, blocks), jnp.int32),
            pltpu.SMEM((subs, blocks), jnp.int32),
            pltpu.VMEM((subs, blocks, S, S), BF),
            pltpu.VMEM((subs, blocks, 2, S), jnp.int32),
            pltpu.VMEM((2, 2, subs, rows, 128), F32),
            pltpu.SMEM((subs,), F32),
            pltpu.SMEM((subs * facets,), jnp.int32),
            pltpu.VMEM((2, facets * pos_rows, S), F32),
            pltpu.VMEM((2, facets, subs * pairs, S, S), BF),
            pltpu.VMEM((facets, vis_rows + pos_rows, 2 * S), BF),
            pltpu.VMEM((facets, halo_rows, 2 * S), BF),
            pltpu.SemaphoreType.DMA((CHUNKS + 8 + 2 * facets,)),
        ],
        compiler_params=params(60),
        name="pack_blocks",
    )(destinations[..., 0], column_slots, visibility, uv_positions, image, dual, steps)


def grid_and_step(received, image, dual, steps, pairs, bands):
    facets = len(received)
    subs, rows, width = image.shape
    vis_rows = subs * pairs * S
    per = 4
    sources = per // pairs
    band_rows = rows // bands
    piece = band_rows + 2 * HALO
    pos_rows = -(-2 * subs * pairs // 16) * 16
    height = 2 * HALO * subs

    def kernel(step_ref, img_ref, dual_ref, *rest):
        rec_refs, rest = rest[:facets], rest[facets:]
        shift_ref, rest = rest[0], rest[1:]
        piece_refs = rest[:bands]
        place_ref, acc_ref, den_ref, halo_ref = rest[bands:]
        for source in range(facets):
            place_ref[source] = rec_refs[source][vis_rows : vis_rows + pos_rows, :].astype(F32)
        one = jnp.ones((), BF)
        none = jnp.zeros((), BF)
        lane = lax.broadcasted_iota(jnp.int32, (1, 2 * S), 1)
        left = jnp.where(lane < S, 1.0, 0.0).astype(BF)
        right = jnp.where(lane < S, 0.0, 1.0).astype(BF)
        zero = jnp.zeros((2 * S, 2 * S), BF)
        row_id = lax.broadcasted_iota(jnp.int32, (rows, 2 * S), 0).astype(F32).astype(BF)
        col_id = (lax.broadcasted_iota(jnp.int32, (width, 2 * S), 0) - CENTRE).astype(F32).astype(BF)

        spreads = [[] for _ in range(subs)]
        hots = [[] for _ in range(subs)]
        for it in range(facets // sources):
            for sub in range(subs):
                first, second = [], []
                for q in range(per):
                    source = it * sources + q // pairs
                    at = sub * pairs + q % pairs
                    block = rec_refs[source][at * S : (at + 1) * S, :]
                    diag = jnp.concatenate([block * left, block * right], axis=0)
                    u_row = place_ref[source, at : at + 1, :].astype(BF)
                    v_row = place_ref[source, at + subs * pairs : at + subs * pairs + 1, :].astype(BF)
                    u_hot = jnp.where(row_id == u_row, one, none)
                    v_hot = jnp.where(col_id == v_row, one, none)
                    first.append((u_hot, diag))
                    second.append(v_hot)
                spread = []
                for q in range(0, per, 2):
                    hot = jnp.concatenate([first[q][0], first[q + 1][0]], axis=1)
                    block = jnp.concatenate(
                        [
                            jnp.concatenate([first[q][1], zero], axis=1),
                            jnp.concatenate([zero, first[q + 1][1]], axis=1),
                        ],
                        axis=0,
                    )
                    spread.append(dot(hot, block).astype(BF))
                spreads[sub] += spread
                hots[sub] += second
                if it % DEPTH == DEPTH - 1:
                    term = contract_last(
                        jnp.concatenate(spreads[sub], axis=1), jnp.concatenate(hots[sub], axis=1)
                    )
                    acc_ref[sub] = term if it < DEPTH else acc_ref[sub] + term
                    spreads[sub], hots[sub] = [], []

        u_taps = tap_matrix(rows)
        v_taps = taps(
            lax.broadcasted_iota(jnp.int32, (width, width), 0),
            lax.broadcasted_iota(jnp.int32, (width, width), 1),
        )
        den_ref[...] = jnp.zeros(den_ref.shape, F32)
        me = lax.axis_index("band")
        for sub in range(subs):
            total = acc_ref[sub]
            half = dot(u_taps, total.astype(BF))
            gradient = dot(half.astype(BF), v_taps)
            stepped = img_ref[sub] - step_ref[sub] * gradient
            shifted = stepped + dual_ref[sub]
            shift_ref[sub] = shifted
            den_ref[sub, HALO : HALO + rows, :] = shifted
        halo = sum(ref[vis_rows + pos_rows :, :].astype(F32) for ref in rec_refs)
        parts = [halo[n * height : (n + 1) * height] for n in range(rows // 128)]
        halo = jnp.concatenate(parts + [jnp.zeros((height, 128), F32)], axis=1)
        steps_in = 128 // band_rows
        for n in range(steps_in):
            shift = (HALO - n * band_rows) % (rows + 128)
            moved = pltpu.roll(halo, shift, 1)
            for tile in range(bands // steps_in):
                halo_ref[tile * steps_in + n] = moved[:, tile * 128 : (tile + 1) * 128]
        blank = jnp.zeros((height, width - 128), F32)
        for k in range(bands):
            band = lax.rem(me + k, bands)
            start = pl.multiple_of(band * band_rows, band_rows)
            piece_refs[k][...] = jnp.concatenate(
                [den_ref[sub, pl.ds(start, piece), :] for sub in range(subs)]
                + [jnp.concatenate([halo_ref[band], blank], axis=1)],
                axis=0,
            ).astype(BF)

    return pl.pallas_call(
        kernel,
        out_shape=[jax.ShapeDtypeStruct(image.shape, F32)]
        + [jax.ShapeDtypeStruct((subs * piece + height, width), BF)] * bands,
        in_specs=[smem()] + [vmem()] * (2 + facets),
        out_specs=[vmem()] * (1 + bands),
        scratch_shapes=[
            pltpu.VMEM((facets, pos_rows, 2 * S), F32),
            pltpu.VMEM((subs, rows, width), F32),
            pltpu.VMEM((subs, rows + 2 * HALO, width), F32),
            pltpu.VMEM((bands, height, 128), F32),
        ],
        compiler_params=params(),
        name="grid_and_step",
    )(steps, image, dual, *received)


def weight_matrices(conv_first, conv_middle, conv_last):
    ci = conv_first.shape[1]
    co = conv_last.shape[0]
    first = conv_first.transpose(3, 2, 1, 0)
    middle = conv_middle.transpose(3, 2, 1, 0)
    last = conv_last[:, :, ::-1].transpose(3, 1, 2, 0).reshape(3, CH, 3 * co)
    ins = GROUP + 2
    outs = GROUP * co

    def kernel(first_ref, mid_ref, last_ref, one_ref, two_ref, three_ref):
        zero = jnp.zeros((ci, CH), F32)
        rows = []
        for t in range(3):
            for r in range(ins):
                parts = []
                for phase in range(2):
                    for k in range(GROUP // 2):
                        dy = r - 2 * k - phase
                        parts.append(first_ref[t, dy].astype(F32) if 0 <= dy < 3 else zero)
                rows.append(jnp.concatenate(parts, axis=1))
        one_ref[...] = jnp.concatenate(rows, axis=0).astype(BF)
        zero = jnp.zeros((CH, CH), BF)
        for t in range(3):
            for r in range(GROUP // 2 + 2):
                parts = [
                    mid_ref[t, r - k] if 0 <= r - k < 3 else zero for k in range(GROUP // 2)
                ]
                at = (t * (GROUP // 2 + 2) + r) * CH
                two_ref[at : at + CH, :] = jnp.concatenate(parts, axis=1)
        three_ref[...] = jnp.zeros(three_ref.shape, BF)
        lane = lax.broadcasted_iota(jnp.int32, (CH, 128), 1)
        keep = jnp.where(lane < outs, 1.0, 0.0)
        for r in range(ins):
            taps = []
            for t in range(3):
                base = jnp.concatenate(
                    [last_ref[t].astype(F32), jnp.zeros((CH, 128 - 3 * co), F32)], axis=1
                )
                taps.append(pltpu.roll(base, (r - 2) * co % 128, 1) * keep)
            block = jnp.concatenate([taps[0] + pltpu.roll(taps[1], outs, 1), taps[2]], axis=1)
            if r < GROUP:
                at = (r % 2 * (GROUP // 2) + r // 2) * CH
            else:
                at = GROUP * CH + (r - GROUP) * 2 * CH
            three_ref[at : at + CH, :] = block.astype(BF)

    return pl.pallas_call(
        kernel,
        out_shape=[
            jax.ShapeDtypeStruct((3 * ins * ci, GROUP * CH), BF),
            jax.ShapeDtypeStruct((3 * (GROUP // 2 + 2) * CH, GROUP // 2 * CH), BF),
            jax.ShapeDtypeStruct(((GROUP + 4) * CH, 256), BF),
        ],
        in_specs=[vmem()] * 3,
        out_specs=[vmem()] * 3,
        compiler_params=params(),
        cost_estimate=pl.CostEstimate(flops=1 << 20, bytes_accessed=1 << 20, transcendentals=0),
        name="weight_matrices",
    )(first, middle, last)


def denoise(pieces, first, middle, last, subs, bands, band_rows, width):
    channels = subs * bands
    piece = band_rows + 2 * HALO
    groups = band_rows // GROUP + 1
    cols = width + 2 * PAD
    lanes = -(-cols // 128) * 128
    tall = -(-(cols + 2 * HALO) // 16) * 16
    in_rows = GROUP + 2
    facets = lax.axis_size("facet")

    def kernel(first_ref, mid_ref, last_ref, *rest):
        piece_refs = rest[:bands]
        out_refs = rest[bands : 2 * bands]
        x_ref, one_ref, two_ref, noise_ref = rest[2 * bands :]
        me = lax.axis_index("band")
        facet = lax.axis_index("facet")
        x_ref[:, piece * channels :, :] = jnp.zeros((lanes // 128, 2 * channels, 128), F32)
        one_ref[groups] = jnp.zeros(one_ref.shape[1:], BF)
        place_row = lax.broadcasted_iota(jnp.int32, (2 * subs * HALO, lanes), 0)
        place_lane = lax.broadcasted_iota(jnp.int32, (2 * subs * HALO, lanes), 1)
        side = place_row // HALO % 2
        spot = jnp.where(side == 0, PAD - HALO, PAD + width) + place_row % HALO
        for k in range(bands):
            band = lax.rem(me + bands - k, bands)
            for sub in range(subs):
                put = jnp.where(
                    (place_lane == spot) & (place_row // (2 * HALO) == sub), 1.0, 0.0
                ).astype(BF)
                halo = contract_first(piece_refs[k][subs * piece :, 0:128], put)[:piece]
                own = piece_refs[k][sub * piece : (sub + 1) * piece, :].astype(F32)
                own = jnp.concatenate([own, jnp.zeros((piece, lanes - width), F32)], axis=1)
                own = pltpu.roll(own, PAD, 1) + halo
                for part in range(lanes // 128):
                    x_ref[part, pl.ds(band * subs + sub, piece, stride=channels), :] = own[
                        :, part * 128 : (part + 1) * 128
                    ]

        col = lax.broadcasted_iota(jnp.int32, (1, lanes), 1) - PAD
        inside = ((col >= 0) | (facet > 0)) & ((col < width) | (facet < facets - 1))
        inside = jnp.where(inside, 1.0, 0.0)
        lane_id = lax.broadcasted_iota(jnp.int32, (1, GROUP * CH), 1)
        lane_row = lane_id // (GROUP // 2 * CH) + 2 * (lane_id // CH % (GROUP // 2))

        def layer_one(g):
            top = g * GROUP * channels
            x = jnp.concatenate(
                [x_ref[part, top : top + in_rows * channels, :] for part in range(lanes // 128)], axis=1
            )
            stack = jnp.concatenate(
                [pltpu.roll(x, 1, 1) * inside, x * inside, pltpu.roll(x, lanes - 1, 1) * inside], axis=0
            )
            stack = stack.astype(BF).T[:cols]
            hidden = dot(stack, first_ref[...])
            row = lane_row + (g * GROUP + 1 - HALO) + me * band_rows
            keep = jnp.where((row >= 0) & (row < band_rows * bands), 1.0, 0.0)
            one_ref[g, 0:cols, :] = (jnp.maximum(hidden, 0.0) * keep).astype(BF)

        block = GROUP // 2 * CH

        def layer_two(g):
            row = lane_row + (g * GROUP - 1) + me * band_rows
            keep = jnp.where((row >= 0) & (row < band_rows * bands), 1.0, 0.0)
            for phase in range(2):
                here = one_ref[g, :, phase * block : (phase + 1) * block]
                after = one_ref[g + 1, :, phase * block : phase * block + 2 * CH]
                parts = []
                for t in range(3):
                    parts += [here[2 * t : 2 * t + cols], after[2 * t : 2 * t + cols]]
                hidden = dot(jnp.concatenate(parts, axis=1), mid_ref[...])
                part = keep[:, phase * block : (phase + 1) * block]
                two_ref[g, :, phase * block : (phase + 1) * block] = (
                    jnp.maximum(hidden, 0.0) * part
                ).astype(BF)

        out_ch = channels * GROUP
        out_col = lax.broadcasted_iota(jnp.int32, (1, width), 1)
        has_left = jnp.where((out_col > 0) | (facet > 0), 1.0, 0.0)
        has_right = jnp.where((out_col < width - 1) | (facet < facets - 1), 1.0, 0.0)

        def layer_three(g):
            hidden = jnp.concatenate(
                [
                    two_ref[g],
                    two_ref[g + 1, :, 0 : 2 * CH],
                    two_ref[g + 1, :, block : block + 2 * CH],
                ],
                axis=1,
            )
            y = dot(hidden, last_ref[...]).T
            base = PAD - 2
            noise = (
                y[:out_ch, base - 1 : base - 1 + width] * has_left
                + y[out_ch : 2 * out_ch, base : base + width]
                + y[2 * out_ch : 3 * out_ch, base + 1 : base + 1 + width] * has_right
            )
            for part in range(width // 128):
                noise_ref[part, g * out_ch : (g + 1) * out_ch, :] = noise[
                    :, part * 128 : (part + 1) * 128
                ]

        for g in range(groups + 4):
            if g < groups:
                layer_one(g)
            if 0 <= g - 2 < groups:
                layer_two(g - 2)
            if 0 <= g - 4 < groups - 1:
                layer_three(g - 4)
        for k in range(bands):
            band = lax.rem(me + k, bands)
            for sub in range(subs):
                for part in range(width // 128):
                    out_refs[k][
                        sub * band_rows : (sub + 1) * band_rows, part * 128 : (part + 1) * 128
                    ] = noise_ref[
                        part, pl.ds(band * subs + sub, band_rows, stride=channels), :
                    ].astype(BF)

    return pl.pallas_call(
        kernel,
        out_shape=[jax.ShapeDtypeStruct((subs * band_rows, width), BF)] * bands,
        in_specs=[vmem()] * (3 + bands),
        out_specs=[vmem()] * bands,
        scratch_shapes=[
            pltpu.VMEM((lanes // 128, (groups * GROUP + 2) * channels, 128), F32),
            pltpu.VMEM((groups + 1, tall, GROUP * CH), BF),
            pltpu.VMEM((groups, cols, GROUP * CH), BF),
            pltpu.VMEM((width // 128, band_rows * channels, 128), F32),
        ],
        compiler_params=params(32),
        name="denoise",
    )(first, middle, last, *pieces)


def finish(shifted, noises, bands):
    subs, rows, width = shifted.shape
    band_rows = rows // bands

    def kernel(shift_ref, *rest):
        noise_refs = rest[:bands]
        img_ref, dual_ref = rest[bands:]
        me = lax.axis_index("band")
        for k in range(bands):
            start = pl.multiple_of(lax.rem(me + bands - k, bands) * band_rows, band_rows)
            for sub in range(subs):
                noise = noise_refs[k][sub * band_rows : (sub + 1) * band_rows, :].astype(F32)
                shifted_part = shift_ref[sub, pl.ds(start, band_rows), :]
                image_next = jnp.maximum(shifted_part - noise, 0.0)
                img_ref[sub, pl.ds(start, band_rows), :] = image_next
                dual_ref[sub, pl.ds(start, band_rows), :] = shifted_part - image_next

    return pl.pallas_call(
        kernel,
        out_shape=[jax.ShapeDtypeStruct(shifted.shape, F32)] * 2,
        in_specs=[vmem()] * (1 + bands),
        out_specs=[vmem()] * 2,
        compiler_params=params(),
        name="finish",
    )(shifted, *noises)


def exchange(parts, bands):
    return [parts[0]] + [
        lax.ppermute(parts[k], "band", [(i, (i + k) % bands) for i in range(bands)])
        for k in range(1, bands)
    ]


def body(
    visibility,
    uv_positions,
    destinations,
    column_slots,
    image_cube,
    dual_cube,
    step_sizes,
    conv_first,
    conv_middle,
    conv_last,
):
    facets = lax.axis_size("facet")
    bands = lax.axis_size("band")
    subs, blocks = visibility.shape[:2]
    rows, width = image_cube.shape[1:]
    pairs = max(2, 2 * blocks // facets) // 2
    packed = pack_blocks(
        visibility,
        uv_positions,
        destinations,
        column_slots,
        image_cube,
        dual_cube,
        step_sizes,
        facets,
        pairs,
    )
    received = [packed[0]] + [
        lax.ppermute(packed[k], "facet", [(i, i ^ k) for i in range(facets)])
        for k in range(1, facets)
    ]
    weights = weight_matrices(conv_first, conv_middle, conv_last)
    shifted, *pieces = grid_and_step(received, image_cube, dual_cube, step_sizes, pairs, bands)
    pieces = exchange(pieces, bands)
    noises = denoise(pieces, *weights, subs, bands, rows // bands, width)
    return tuple(finish(shifted, exchange(noises, bands), bands))


def solution(mesh):
    return jax.shard_map(
        body,
        mesh=mesh,
        in_specs=(
            P("band", "facet", None, None),
            P("band", "facet", None, None),
            P("band", "facet", None),
            P("band", "facet"),
            P("band", None, "facet"),
            P("band", None, "facet"),
            P("band"),
            P(),
            P(),
            P(),
        ),
        out_specs=(P("band", None, "facet"), P("band", None, "facet")),
        check_vma=False,
    )
```
